32 devices in a mesh: gx: 8 (over y, x, core), gy: 4 (over z).
Axes of the slice: x: 2, y: 2, z: 4, core: 2. Of those that a mesh axis runs over, the one named last changes fastest.
Arguments:
- ocean_depth: float32 [2048, 2048], P('gx', 'gy'), may hold values from 0.5 to 8
- wet_mask: int32 [2048, 2048], P('gx', 'gy'), may hold values 0 or 1
- manning: float32 [2048, 2048], P('gx', 'gy'), may hold values from 0.5 to 5
- fault_slip: float32 [512], P(('gx', 'gy')), may hold values from 0.3 to 1.2
- pattern: float32 [8192, 8, 128], P(('gx', 'gy')), may hold values from -1 to 1
- foot_tile: int32 [8192, 1], P(('gx', 'gy')), may hold values from 0 to 31; in each aligned block of 256 rows (0 to 255, 256 to 511, ...) at most 16 rows name the same one
- foot_block: int32 [8192], P(('gx', 'gy')), may hold values from 0 to 127
- gauge_row: int32 [512], replicated, may hold values from 0 to 2047, as said below
- gauge_col: int32 [512], replicated, may hold values from 0 to 2047, as said below
- observed: float32 [4, 512], replicated, may hold values from -6 to 6
Outputs:
- final_eta: float32 [2048, 2048], P('gx', 'gy')
- readings: float32 [4, 512], replicated
- source_adjoint: float32 [2048, 2048], P('gx', 'gy')
- grad_slip: float32 [512], P(('gx', 'gy'))
The draws below stay inside these ranges and needn't reach their ends.
Inputs may be any that keep to these rules, and one draw needn't show every extreme that they name: `foot_tile`: the 256 rows of one device name no tile more than 16 times, a bound that some block reaches. Tile t is the one at tile row t // 4 and tile column t % 4. `gauge_row`: gauges 16 * t to 16 * t + 15 lie in tile t, within three cells of one of its edges. `gauge_col`: see gauge_row.
All inputs are finite; a program needn't handle non-finite values. No bound on the sum of `wet_mask` on one device may be relied on, other than what follows from the above.
Results may differ from the reference program's by a relative error of at most 0.0003.
Values sent between devices are 32-bit elements; how exact they have to be, the bound alone decides.
A program may use at most 128 MiB of HBM per device.

```python
import math
from functools import partial
import jax
import jax.numpy as jnp
import numpy as np

CR = 256
CC = 512
SUB_DEV = 16
FP = 16
GAUGE_DEV = 16
STEPS = 4
GRID_R = 2048
GRID_C = 2048
TILES_C = 4
NB = 128
SUB = 512
GAUGES = 512
CAP = 16
DEVICES = 32


def gauge_places(key):
    base = jax.random.fold_in(key, 41)
    first_key, second_key = jax.random.split(base)
    numbers = jnp.arange(GAUGES, dtype=jnp.int32)
    tile_index = numbers // GAUGE_DEV
    edge_side = numbers % 4
    inset = jax.random.randint(first_key, (GAUGES,), 0, 3, dtype=jnp.int32)
    along = jax.random.randint(second_key, (GAUGES,), 0, 1 << 20, dtype=jnp.int32)
    local_row = jnp.where(edge_side == 0, inset, jnp.where(edge_side == 1, CR - 1 - inset, along % CR))
    local_col = jnp.where(edge_side == 2, inset, jnp.where(edge_side == 3, CC - 1 - inset, along % CC))
    tiles_across = GRID_C // CC
    grid_row = tile_index // tiles_across * CR + local_row
    grid_col = tile_index % tiles_across * CC + local_col
    return (grid_row.astype(jnp.int32), grid_col.astype(jnp.int32))


def draw_gauge_row(key, part):
    return gauge_places(key)[0]


def draw_gauge_col(key, part):
    return gauge_places(key)[1]


def touch_ends(drawn, own_key, least, largest):
    longest = drawn.shape.index(max(drawn.shape))
    spots = []
    for shift in (0, 1):
        where = [jax.random.randint(jax.random.fold_in(own_key, axis), (), 0, length) for axis, length in enumerate(drawn.shape)]
        where[longest] = (where[longest] + shift) % drawn.shape[longest]
        spots.append(tuple(where))
    return drawn.at[spots[0]].set(least).at[spots[1]].set(largest)


def block_scale(stream_key, shape, pieces, low, top_value):
    loudness = 1.0
    for dim, parts in pieces:
        heights = jax.random.uniform(jax.random.fold_in(jax.random.fold_in(stream_key, 6), dim), (parts,), jnp.float32, low / len(pieces), top_value / len(pieces))
        loudness = loudness * jnp.repeat(jnp.exp(heights), shape[dim] // parts).reshape((-1,) + (1,) * (len(shape) - 1 - dim))
    return loudness


def shared_out(own_key, own, number, rows, count, top, bound, skew):
    order = jax.random.permutation(own_key, count)
    crowded, common = portions_of(count, rows * top, bound, skew, True), portions_of(count, rows * top, bound, skew, False)
    places = jnp.arange(count)

    def named(lengths, offset_by):
        used = int((lengths > 0).sum())
        fixed = max(1, used // 4)
        passed = fixed + (places - fixed + offset_by * (used - fixed)) % max(1, count - fixed)
        return jnp.zeros((count,), jnp.int32).at[order[jnp.where(places < fixed, places, passed)]].set(jnp.asarray(lengths, jnp.int32))

    lengths = jnp.where(number % 4 == 0, named(crowded, number // 4), named(common, number - number // 4 - 1))
    mixed = jax.random.permutation(jax.random.fold_in(own, 3), count)
    source_of, taker = mixed[0:count // 2 * 2:2], mixed[1:count // 2 * 2:2]
    room = jnp.minimum(lengths[source_of] - 1, bound - lengths[taker]) // 2
    room = jnp.where((source_of == order[0]) | (taker == order[0]) | (lengths[taker] == 0), 0, jnp.maximum(room, 0))
    passed = jax.random.randint(jax.random.fold_in(own, 4), (count // 2,), 0, 1 << 20) % (room + 1)
    lengths = lengths.at[source_of].add(-passed).at[taker].add(passed)
    items = jnp.searchsorted(jnp.cumsum(lengths), jnp.arange(rows * top), side="right").astype(jnp.int32)
    grid = items.reshape(top, rows).T
    grid = grid[jax.random.permutation(jax.random.fold_in(own, 1), rows)]
    offset_by = jax.random.randint(jax.random.fold_in(own, 2), (rows, 1), 0, top)
    return jnp.take_along_axis(grid, (jnp.arange(top)[None, :] + offset_by) % top, axis=1)


def portions_of(amount, total, reach, lean, full):
    portions = [(1 << 20) // math.isqrt(standing ** lean) + 1 for standing in range(1, amount + 1)]
    largest = reach if full else min(reach, max(-(-total // amount), total * portions[0] // sum(portions)))
    least = 1 if total - largest >= amount - 1 else 0
    counts, spare = [largest] + [least] * (amount - 1), total - largest - least * (amount - 1)
    while spare > 0:
        candidates = [i for i in range(1, amount) if counts[i] < largest] or [i for i in range(1, amount) if counts[i] < reach]
        mass, remaining = sum([portions[i] for i in candidates]), spare
        for i in candidates:
            more = min(reach - counts[i], max(1, remaining * portions[i] // mass), spare)
            counts[i] = counts[i] + more
            spare = spare - more
    return np.array(counts)


def normal_values(key, shape, deviation, reach, kind=jnp.bfloat16):
    entries = jax.random.normal(key, shape, jnp.float32) * deviation
    return jnp.minimum(jnp.maximum(entries, -reach), reach).astype(kind)


def setup_inputs(seed: int = 0) -> dict:
    seeds = jax.random.split(jax.random.key(seed), 11)
    ocean_depth = jnp.clip(jnp.exp(math.log(8.0) - 2.7725887 * jax.random.uniform(seeds[0], (GRID_R, GRID_C), jnp.float32) ** block_scale(seeds[0], (GRID_R, GRID_C), ((0, 8), (1, 4)), -0.2, 0.2)), 0.5, 8.0)
    wet_mask = touch_ends((jax.random.randint(seeds[1], (GRID_R, GRID_C), 0, 8) < 7).astype(jnp.int32), jax.random.fold_in(seeds[1], 1), 0, 1)
    manning = jnp.clip(jnp.exp(math.log(5.0) - 2.3025851 * jax.random.uniform(seeds[2], (GRID_R, GRID_C), jnp.float32) ** block_scale(seeds[2], (GRID_R, GRID_C), ((0, 8), (1, 4)), -0.2, 0.2)), 0.5, 5.0)
    fault_slip = jnp.clip(jnp.exp(math.log(1.2) - 1.3862944 * jax.random.uniform(seeds[3], (SUB,), jnp.float32) ** block_scale(seeds[3], (SUB,), ((0, 32),), -0.2, 0.2)), 0.3, 1.2)
    pattern = jnp.clip(jax.random.uniform(seeds[4], (SUB * FP, 8, 128), jnp.float32, -1.0, 1.0) * block_scale(seeds[4], (SUB * FP, 8, 128), ((0, 32),), -0.4, 0.0), -1.0, 1.0)
    foot_tile_keys = jax.random.split(jax.random.fold_in(seeds[5], 1), (SUB * FP) // (SUB_DEV * FP))
    foot_tile_turns = jax.random.permutation(jax.random.fold_in(seeds[5], 3), (SUB * FP) // (SUB_DEV * FP))
    foot_tile = jax.vmap(lambda own, number: shared_out(jax.random.fold_in(seeds[5], 2), own, number, SUB_DEV * FP, DEVICES, 1, CAP, 2))(foot_tile_keys, foot_tile_turns).reshape((SUB * FP, 1))
    foot_block = touch_ends(jax.random.randint(seeds[6], (SUB * FP,), 0, NB), jax.random.fold_in(seeds[6], 1), 0, NB - 1).astype(jnp.int32)
    gauge_row = draw_gauge_row(jax.random.fold_in(seeds[10], 71), 0)
    gauge_col = draw_gauge_col(jax.random.fold_in(seeds[10], 71), 0)
    observed = normal_values(seeds[9], (STEPS, GAUGES), 1.0, 6.0, jnp.float32)
    return {"ocean_depth": ocean_depth, "wet_mask": wet_mask, "manning": manning, "fault_slip": fault_slip, "pattern": pattern, "foot_tile": foot_tile, "foot_block": foot_block, "gauge_row": gauge_row, "gauge_col": gauge_col, "observed": observed}


wave_gain = 0.2
mass_gain = 0.2
min_depth = 0.25
speed_floor = 0.01

def eastward(field, column):
    return jnp.concatenate([field[:, 1:], column[:, None]], axis=1)

def southward(field, row_edge):
    return jnp.concatenate([field[1:], row_edge[None]], axis=0)

def face_flux(flux, here, there, depth_here, depth_there, wet_here, wet_there, fric_here, fric_there):
    total_depth = jnp.maximum(0.5 * (depth_here + here + depth_there + there), min_depth)
    pushed = flux - wave_gain * total_depth * (there - here)
    roughness = 0.5 * (fric_here + fric_there)
    drag_factor = 1.0 + roughness * jnp.sqrt(pushed * pushed + speed_floor) / jnp.power(total_depth, 7.0 / 3.0)
    return wet_here * wet_there * pushed / drag_factor

def fluxes(statics, static_east, static_south, surface, east_rim, south_rim, flux_east, flux_south):
    depth_here, wet_here, fric_here = (statics[0], statics[1], statics[2])
    next_east = face_flux(flux_east, surface, eastward(surface, east_rim), depth_here, eastward(depth_here, static_east[0]), wet_here, eastward(wet_here, static_east[1]), fric_here, eastward(fric_here, static_east[2]))
    next_south = face_flux(flux_south, surface, southward(surface, south_rim), depth_here, southward(depth_here, static_south[0]), wet_here, southward(wet_here, static_south[1]), fric_here, southward(fric_here, static_south[2]))
    return (next_east, next_south)

def surface_step(wet_cells, surface, next_east, next_south, west_rim, north_rim):
    left_flux = jnp.concatenate([west_rim[:, None], next_east[:, :-1]], axis=1)
    upper_flux = jnp.concatenate([north_rim[None], next_south[:-1]], axis=0)
    return wet_cells * (surface - mass_gain * (next_east - left_flux + next_south - upper_flux))

def tile_from_blocks(blocks, rows_here, cols_here):
    return blocks.reshape(rows_here // 8, cols_here // 128, 8, 128).transpose(0, 2, 1, 3).reshape(rows_here, cols_here)

def build_source(fault_slip, pattern, foot_tile, foot_block, wet_cells):
    tile_index = foot_tile[:, 0]
    per_row = CC // 128
    block_row = tile_index // TILES_C * (CR // 8) + foot_block // per_row
    block_col = tile_index % TILES_C * per_row + foot_block % per_row
    global_block = block_row * (GRID_C // 128) + block_col
    weights = jnp.repeat(fault_slip, FP)
    terms = weights[:, None] * pattern.reshape(SUB * FP, 1024)
    grid_blocks = jnp.zeros((GRID_R // 8 * (GRID_C // 128), 1024), jnp.float32).at[global_block].add(terms)
    return tile_from_blocks(grid_blocks, GRID_R, GRID_C) * wet_cells

def reference(ocean_depth, wet_mask, manning, fault_slip, pattern, foot_tile, foot_block, gauge_row, gauge_col, observed):
    wet_cells = wet_mask.astype(jnp.float32)
    statics = jnp.stack([ocean_depth, wet_cells, manning])
    zero_cols = jnp.zeros((3, GRID_R), jnp.float32)
    zero_rows = jnp.zeros((3, GRID_C), jnp.float32)
    edge_col = jnp.zeros((GRID_R,), jnp.float32)
    edge_row = jnp.zeros((GRID_C,), jnp.float32)

    def run(eta_start):
        surface = eta_start
        flux_east = jnp.zeros_like(eta_start)
        flux_south = jnp.zeros_like(eta_start)
        gathered = []
        for step_index in range(STEPS):
            next_east, next_south = fluxes(statics, zero_cols, zero_rows, surface, edge_col, edge_row, flux_east, flux_south)
            surface = surface_step(wet_cells, surface, next_east, next_south, edge_col, edge_row)
            flux_east, flux_south = (next_east, next_south)
            gathered.append(surface[gauge_row, gauge_col])
        return (surface, jnp.stack(gathered))
    eta_start, source_fn = jax.vjp(partial(build_source, pattern=pattern, foot_tile=foot_tile, foot_block=foot_block, wet_cells=wet_cells), fault_slip)
    (final_eta, readings), run_fn = jax.vjp(run, eta_start)
    misfit_terms = readings - observed
    source_adjoint, = run_fn((jnp.zeros_like(final_eta), misfit_terms))
    grad_slip, = source_fn(source_adjoint)
    return (final_eta, readings, source_adjoint, grad_slip)
```

```python
from functools import partial

import jax
import jax.numpy as jnp
from jax import lax
from jax.experimental import pallas as pl
from jax.experimental.pallas import tpu as pltpu
from jax.sharding import PartitionSpec as P

wave_gain = 0.2
mass_gain = 0.2
min_depth = 0.25
speed_floor = 0.01
LANES = 128
SUBL = 8


def shifted(shard, axis, by):
    devices = lax.axis_size(axis)
    pairs = [(i, i + by) for i in range(devices) if 0 <= i + by < devices]
    return lax.ppermute(shard, axis, pairs)


def widen(field, halo, wide):
    cols = field.shape[-1]
    east = shifted(field[..., :halo], "gy", -1)
    west = shifted(field[..., cols - halo :], "gy", 1)
    gap = jnp.zeros(field.shape[:-1] + (wide - cols - 2 * halo,), field.dtype)
    field = jnp.concatenate([field, east, gap, west], axis=-1)
    rows = field.shape[-2]
    south = shifted(field[..., :halo, :], "gx", -1)
    north = shifted(field[..., rows - halo :, :], "gx", 1)
    return jnp.concatenate([north, field, south], axis=-2)


def source_kernel(blocks_ref, recv_ref, wet_ref, out_ref, *, capacity, per_row):
    out_ref[...] = jnp.zeros_like(out_ref)

    def add(s, _):
        b = blocks_ref[s]
        r = pl.multiple_of(b // per_row * SUBL, SUBL)
        c = pl.multiple_of(b % per_row * LANES, LANES)
        here = (pl.ds(r, SUBL), pl.ds(c, LANES))
        out_ref[here] += recv_ref[s // capacity, s % capacity]
        return _

    lax.fori_loop(0, blocks_ref.shape[0], add, 0)
    out_ref[...] = out_ref[...] * wet_ref[...].astype(jnp.float32)


def steps_kernel(
    blocks_ref,
    grow_ref,
    gcol_ref,
    start_ref,
    static_ref,
    gauge_ref,
    recv_ref,
    final_ref,
    adjoint_ref,
    slot_ref,
    read_ref,
    face_ref,
    surf_ref,
    flux_ref,
    coef_ref,
    lam_ref,
    pick_ref,
    *,
    steps,
    halo,
    capacity,
):
    high, wide = start_ref.shape
    rows, cols = final_ref.shape
    strips = high // SUBL
    per_row = cols // LANES
    line = lax.broadcasted_iota(jnp.int32, (SUBL, wide), 0)

    def at(i):
        return pl.ds(pl.multiple_of(i * SUBL, SUBL), SUBL)

    def after(i):
        return at(jnp.minimum(i + 1, strips - 1))

    def east(x):
        return pltpu.roll(x, wide - 1, 1)

    def west(x):
        return pltpu.roll(x, 1, 1)

    def south(x, below):
        return jnp.where(line == SUBL - 1, pltpu.roll(below, SUBL - 1, 0), pltpu.roll(x, SUBL - 1, 0))

    def north(x, above):
        return jnp.where(line == 0, pltpu.roll(above, 1, 0), pltpu.roll(x, 1, 0))

    zero = jnp.zeros((SUBL, wide), jnp.float32)

    def prepare(i, _):
        here, below = at(i), after(i)
        depth, wet, fric = (static_ref[n, here, :] for n in range(3))
        depth_b, wet_b, fric_b = (static_ref[n, below, :] for n in range(3))
        face_ref[0, here, :] = 0.5 * (depth + east(depth))
        face_ref[1, here, :] = wet * east(wet)
        face_ref[2, here, :] = 0.5 * (fric + east(fric))
        face_ref[3, here, :] = 0.5 * (depth + south(depth, depth_b))
        face_ref[4, here, :] = wet * south(wet, wet_b)
        face_ref[5, here, :] = 0.5 * (fric + south(fric, fric_b))
        return _

    lax.fori_loop(0, strips, prepare, 0)

    def face(flux, here, there, depth, wet, rough):
        raw = depth + 0.5 * (here + there)
        total = jnp.maximum(raw, min_depth)
        slope = there - here
        pushed = flux - wave_gain * total * slope
        square = pushed * pushed
        inv_speed = lax.rsqrt(square + speed_floor)
        speed = (square + speed_floor) * inv_speed
        logd = jnp.log(total)
        drag = rough * jnp.exp(logd * (-7.0 / 3.0))
        inv_depth = jnp.exp(-logd)
        ds = drag * speed
        inv = 1.0 / (1.0 + ds)
        wi = wet * inv
        out = wi * pushed
        d_push = wi * (1.0 - drag * square * inv_speed * inv)
        d_total = (7.0 / 3.0) * out * ds * inv * inv_depth - wave_gain * slope * d_push
        half = jnp.where(raw > min_depth, 0.5, jnp.where(raw == min_depth, 0.25, 0.0))
        both = half * d_total
        apart = wave_gain * total * d_push
        return out, d_push, apart + both, both - apart

    for k in range(steps):
        old = start_ref if k == 0 else surf_ref.at[k - 1]

        def forward(i, carry, k=k, old=old):
            cur, flux_above = carry
            here = at(i)
            nxt = old[after(i), :]
            fe = zero if k == 0 else flux_ref[0, here, :]
            fs = zero if k == 0 else flux_ref[1, here, :]
            ne, ae, xe, ye = face(
                fe, cur, east(cur), face_ref[0, here, :], face_ref[1, here, :], face_ref[2, here, :]
            )
            if k:
                coef_ref[k, 0, here, :] = ae
            coef_ref[k, 1, here, :] = xe
            coef_ref[k, 2, here, :] = ye
            ns, a_s, xs, ys = face(
                fs, cur, south(cur, nxt), face_ref[3, here, :], face_ref[4, here, :], face_ref[5, here, :]
            )
            if k:
                coef_ref[k, 3, here, :] = a_s
            coef_ref[k, 4, here, :] = xs
            coef_ref[k, 5, here, :] = ys
            if k < steps - 1:
                flux_ref[0, here, :] = ne
                flux_ref[1, here, :] = ns
            moved = ne - west(ne) + ns - north(ns, flux_above)
            surf_ref[k, here, :] = static_ref[1, here, :] * (cur - mass_gain * moved)
            return nxt, ns

        lax.fori_loop(0, strips, forward, (old[at(0), :], zero))

    final_ref[...] = surf_ref[steps - 1, halo : halo + rows, :cols]
    mine = grow_ref.shape[0]
    lane = lax.broadcasted_iota(jnp.int32, (mine, wide), 1)
    for k in range(steps):
        for g in range(mine):
            pick_ref[pl.ds(g, 1), :] = surf_ref[k, pl.ds(grow_ref[g], 1), :]
        hit = jnp.where(lane == gcol_ref[...], pick_ref[...], 0.0)
        read_ref[k] = jnp.broadcast_to(jnp.sum(hit, axis=1, keepdims=True), read_ref.shape[1:])

    for k in reversed(range(steps)):
        last = k == steps - 1
        src, dst = lam_ref.at[(k + 1) % 2], lam_ref.at[k % 2]

        def seeded(where, k=k, last=last, src=src):
            seed = gauge_ref[0, where, :] * surf_ref[k, where, :] - gauge_ref[1 + k, where, :]
            total = seed if last else src[where, :] + seed
            return static_ref[1, where, :] * total

        def backward(i, carry, k=k, last=last, dst=dst, seeded=seeded):
            cur, above = carry
            here = at(i)
            nxt = seeded(after(i))
            ge = -mass_gain * (cur - east(cur))
            gs = -mass_gain * (cur - south(cur, nxt))
            if not last:
                ge = ge + flux_ref[0, here, :]
                gs = gs + flux_ref[1, here, :]
            if k:
                flux_ref[0, here, :] = ge * coef_ref[k, 0, here, :]
                flux_ref[1, here, :] = gs * coef_ref[k, 3, here, :]
            ve = ge * coef_ref[k, 2, here, :]
            vs = gs * coef_ref[k, 5, here, :]
            dst[here, :] = (
                cur
                + ge * coef_ref[k, 1, here, :]
                + west(ve)
                + gs * coef_ref[k, 4, here, :]
                + north(vs, above)
            )
            return nxt, vs

        lax.fori_loop(0, strips, backward, (seeded(at(0)), zero))

    adjoint_ref[...] = lam_ref[0, halo : halo + rows, :cols]
    lam_ref[1, halo : halo + rows, :cols] = (
        adjoint_ref[...] * static_ref[1, halo : halo + rows, :cols]
    )

    def dots(d, _):
        for j in range(capacity):
            s = d * capacity + j
            b = blocks_ref[s]
            r = pl.multiple_of(b // per_row * SUBL + halo, SUBL)
            c = pl.multiple_of(b % per_row * LANES, LANES)
            prod = lam_ref[1, pl.ds(r, SUBL), pl.ds(c, LANES)] * recv_ref[d, j]
            slot_ref[d, pl.ds(j, 1), :] = jnp.sum(prod, axis=0, keepdims=True)
        return _

    lax.fori_loop(0, recv_ref.shape[0], dots, 0)


def body(
    ocean_depth,
    wet_mask,
    manning,
    fault_slip,
    pattern,
    foot_tile,
    foot_block,
    gauge_row,
    gauge_col,
    observed,
):
    rows, cols = ocean_depth.shape
    steps = observed.shape[0]
    halo = -(-2 * steps // SUBL) * SUBL
    wide = -(-(cols + 2 * halo) // LANES) * LANES
    high = rows + 2 * halo
    width_x = lax.axis_size("gx")
    width_y = lax.axis_size("gy")
    devices = width_x * width_y
    entries = pattern.shape[0]
    per_fault = entries // fault_slip.shape[0]
    capacity = max(2, (2 * entries + devices - 1) // devices)
    per_row = cols // LANES
    f32 = jnp.float32

    target = foot_tile[:, 0]
    order = jnp.arange(entries, dtype=jnp.int32)
    earlier = (target[:, None] == target[None, :]) & (order[:, None] > order[None, :])
    rank = jnp.sum(earlier.astype(jnp.int32), axis=1)
    place = target * capacity + rank
    weights = jnp.repeat(fault_slip, per_fault)
    send_place = target * (capacity + 1) + rank
    is_slot = place[:, None] == jnp.arange(devices * capacity, dtype=jnp.int32)[None, :]
    slot_block = jnp.sum(jnp.where(is_slot, foot_block[:, None], 0), axis=0).astype(f32)
    head = jnp.zeros((devices, SUBL, LANES), f32).at[:, 0, :capacity].set(
        slot_block.reshape(devices, capacity)
    )
    out_rows = (
        jnp.zeros((devices * (capacity + 1), SUBL, LANES), f32)
        .at[send_place]
        .set(pattern * weights[:, None, None])
        .reshape(devices, capacity + 1, SUBL, LANES)
        .at[:, capacity]
        .set(head)
    )
    recv = lax.all_to_all(out_rows, ("gx", "gy"), split_axis=0, concat_axis=0, tiled=True)
    blocks = recv[:, capacity, 0, :capacity].astype(jnp.int32).reshape(-1)

    here_x, here_y = lax.axis_index("gx"), lax.axis_index("gy")
    wet = wet_mask.astype(f32)
    statics = widen(jnp.stack([ocean_depth, wet, manning]), halo, wide)
    local_row = gauge_row - here_x * rows + halo
    local_col = gauge_col - here_y * cols
    local_col = jnp.where(
        (local_col < -halo) | (local_col >= cols + halo), -1, (local_col + wide) % wide
    )
    row_hot = (jnp.arange(high, dtype=jnp.int32)[:, None] == local_row[None, :]).astype(f32)
    col_hot = (local_col[:, None] == jnp.arange(wide, dtype=jnp.int32)[None, :]).astype(f32)
    values = jnp.concatenate([jnp.ones_like(observed[:1]), observed], axis=0)
    gauges = lax.dot_general(
        (values[:, None, :] * row_hot[None]).reshape(-1, values.shape[1]),
        col_hot,
        (((1,), (0,)), ((), ())),
        precision=lax.Precision.HIGHEST,
        preferred_element_type=f32,
    ).reshape(steps + 1, high, wide)
    mine = gauge_row.shape[0] // devices
    me = here_x * width_y + here_y
    my_row = lax.dynamic_slice_in_dim(local_row, me * mine, mine)
    my_col = lax.dynamic_slice_in_dim(local_col, me * mine, mine)

    vmem = pl.BlockSpec(memory_space=pltpu.VMEM)
    smem = pl.BlockSpec(memory_space=pltpu.SMEM)
    params = pltpu.CompilerParams(vmem_limit_bytes=52 * 1024 * 1024)
    start = pl.pallas_call(
        partial(source_kernel, capacity=capacity, per_row=per_row),
        out_shape=jax.ShapeDtypeStruct((rows, cols), f32),
        in_specs=[smem, vmem, vmem],
        out_specs=vmem,
        compiler_params=params,
    )(blocks, recv, wet_mask)
    start = widen(start, halo, wide)
    final_eta, adjoint, per_slot, reads = pl.pallas_call(
        partial(steps_kernel, steps=steps, halo=halo, capacity=capacity),
        out_shape=(
            jax.ShapeDtypeStruct((rows, cols), f32),
            jax.ShapeDtypeStruct((rows, cols), f32),
            jax.ShapeDtypeStruct((devices, capacity, LANES), f32),
            jax.ShapeDtypeStruct((steps, mine, LANES), f32),
        ),
        in_specs=[smem, smem, vmem, vmem, vmem, vmem, vmem],
        out_specs=(vmem, vmem, vmem, vmem),
        scratch_shapes=[
            pltpu.VMEM((6, high, wide), f32),
            pltpu.VMEM((steps, high, wide), f32),
            pltpu.VMEM((2, high, wide), f32),
            pltpu.VMEM((steps, 6, high, wide), f32),
            pltpu.VMEM((2, high, wide), f32),
            pltpu.VMEM((mine, wide), f32),
        ],
        compiler_params=params,
    )(blocks, my_row, my_col[:, None], start, statics, gauges, recv)
    told = jnp.concatenate(
        [
            jnp.sum(per_slot, axis=2),
            jnp.broadcast_to(reads[:, :, 0].reshape(1, -1), (devices, steps * mine)),
        ],
        axis=1,
    )
    heard = lax.all_to_all(told, ("gx", "gy"), split_axis=0, concat_axis=0, tiled=True)
    readings = heard[:, capacity:].reshape(devices, steps, mine)
    readings = readings.transpose(1, 0, 2).reshape(steps, devices * mine)
    per_entry = jnp.sum(jnp.where(is_slot, heard[:, :capacity].reshape(1, -1), 0.0), axis=1)
    grad_slip = jnp.sum(per_entry.reshape(-1, per_fault), axis=1) / fault_slip
    return (final_eta, readings, adjoint, grad_slip)


def solution(mesh):
    placed = (
        P("gx", "gy"),
        P("gx", "gy"),
        P("gx", "gy"),
        P(("gx", "gy")),
        P(("gx", "gy"), None, None),
        P(("gx", "gy"), None),
        P(("gx", "gy")),
        P(),
        P(),
        P(),
    )
    return jax.shard_map(
        body,
        mesh=mesh,
        in_specs=placed,
        out_specs=(P("gx", "gy"), P(), P("gx", "gy"), P(("gx", "gy"))),
        check_vma=False,
    )
```

```python
from functools import partial

import jax
import jax.numpy as jnp
from jax import lax
from jax.experimental import pallas as pl
from jax.experimental.pallas import tpu as pltpu
from jax.sharding import PartitionSpec as P

wave_gain = 0.2
mass_gain = 0.2
min_depth = 0.25
speed_floor = 0.01
LANES = 128
SUBL = 8


def partner_of(number, width_y):
    return {"gx": number // width_y, "gy": lax.rem(number, width_y)}


def greet_all(me, devices, width_y):
    barrier = pltpu.get_barrier_semaphore()

    def greet(o, _):
        other = partner_of(lax.rem(me + o, devices), width_y)
        pl.semaphore_signal(barrier, inc=1, device_id=other, device_id_type=pl.DeviceIdType.MESH)
        return _

    lax.fori_loop(1, devices, greet, 0)
    pl.semaphore_wait(barrier, devices - 1)


def pack(x, first, halo):
    parts = LANES // halo
    per = x.shape[0] // parts
    group = lax.broadcasted_iota(jnp.int32, (per, LANES), 1) // halo
    out = jnp.zeros((per, LANES), x.dtype)
    for c in range(parts):
        by = (c * halo - first) % LANES
        part = x[c * per : (c + 1) * per]
        out = jnp.where(group == c, pltpu.roll(part, by, 1) if by else part, out)
    return out


def unpack(x, first, halo):
    lane = lax.broadcasted_iota(jnp.int32, x.shape, 1)
    inside = (lane >= first) & (lane < first + halo)
    out = []
    for c in range(LANES // halo):
        by = (first - c * halo) % LANES
        out.append(jnp.where(inside, pltpu.roll(x, by, 1) if by else x, 0.0))
    return jnp.concatenate(out, axis=0)


class Rim:
    def __init__(self, ext_ref, out_buf, in_buf, send_sem, recv_sem, rows, cols, halo):
        self.ext, self.out, self.inn = ext_ref, out_buf, in_buf
        self.rows, self.cols, self.halo = rows, cols, halo
        x, y = lax.axis_index("gx"), lax.axis_index("gy")
        self.has = (
            y > 0,
            y < lax.axis_size("gy") - 1,
            x > 0,
            x < lax.axis_size("gx") - 1,
        )
        self.to = ({"gy": y - 1}, {"gy": y + 1}, {"gx": x - 1}, {"gx": x + 1})
        low, end = halo, halo + rows
        ends = (
            (out_buf.at[0], in_buf.at[1]),
            (out_buf.at[1], in_buf.at[0]),
            (ext_ref.at[:, low : low + halo, :], ext_ref.at[:, end : end + halo, :]),
            (ext_ref.at[:, end - halo : end, :], ext_ref.at[:, 0:halo, :]),
        )
        back = (1, 0, 3, 2)
        self.copies = [
            pltpu.make_async_remote_copy(
                src_ref=ends[d][0],
                dst_ref=ends[d][1],
                send_sem=send_sem.at[d],
                recv_sem=recv_sem.at[back[d]],
                device_id=self.to[d],
                device_id_type=pl.DeviceIdType.MESH,
            )
            for d in range(4)
        ]
        self.back = back

    def greet(self):
        barrier = pltpu.get_barrier_semaphore()
        for has, to in zip(self.has, self.to):

            @pl.when(has)
            def _(to=to):
                pl.semaphore_signal(
                    barrier, inc=1, device_id=to, device_id_type=pl.DeviceIdType.MESH
                )

        pl.semaphore_wait(barrier, sum(has.astype(jnp.int32) for has in self.has))

    def pack_columns(self):
        inner = slice(self.halo, self.halo + self.rows)
        for f in range(self.ext.shape[0]):
            self.out[0, f] = pack(self.ext[f, inner, :LANES], 0, self.halo)
            self.out[1, f] = pack(
                self.ext[f, inner, self.cols - LANES : self.cols], LANES - self.halo, self.halo
            )

    def start(self, d):
        @pl.when(self.has[d])
        def _():
            self.copies[d].start()

    def finish(self, d):
        @pl.when(self.has[d])
        def _():
            self.copies[self.back[d]].wait_recv()

        @pl.when(jnp.logical_not(self.has[d]))
        def _():
            if d < 2:
                self.inn[d] = jnp.zeros(self.inn.shape[1:], jnp.float32)
            else:
                at = 0 if d == 2 else self.halo + self.rows
                self.ext[:, at : at + self.halo, :] = jnp.zeros(
                    (self.ext.shape[0], self.halo, self.ext.shape[2]), jnp.float32
                )

    def turn(self):
        self.finish(0)
        self.finish(1)
        inner = slice(self.halo, self.halo + self.rows)
        for f in range(self.ext.shape[0]):
            self.ext[f, inner, self.cols :] = unpack(self.inn[1, f], 0, self.halo) + unpack(
                self.inn[0, f], LANES - self.halo, self.halo
            )
        self.start(2)
        self.start(3)

    def end(self):
        self.finish(2)
        self.finish(3)
        for d in range(4):

            @pl.when(self.has[d])
            def _(d=d):
                self.copies[d].wait_send()


def spread_kernel(
    row_ref,
    weight_ref,
    pattern_ref,
    head_ref,
    depth_ref,
    wet_ref,
    fric_ref,
    grow_ref,
    gcol_ref,
    value_ref,
    recv_ref,
    static_ref,
    gauge_ref,
    send_ref,
    out_buf,
    in_buf,
    send_sem,
    recv_sem,
    rim_send,
    rim_recv,
    *,
    halo,
    capacity,
):
    rows, cols = depth_ref.shape
    high, wide = static_ref.shape[1:]
    width_y = lax.axis_size("gy")
    devices = lax.axis_size("gx") * width_y
    me = lax.axis_index("gx") * width_y + lax.axis_index("gy")
    rim = Rim(static_ref, out_buf, in_buf, rim_send, rim_recv, rows, cols, halo)
    for f, ref in enumerate((depth_ref, wet_ref, fric_ref)):
        static_ref[f, halo : halo + rows, :cols] = ref[...].astype(jnp.float32)
    rim.pack_columns()
    greet_all(me, devices, width_y)
    rim.start(0)
    rim.start(1)

    def fill(dst, p):
        for j in range(capacity):
            s = p * (capacity + 1) + j
            dst[j] = pattern_ref[row_ref[s]] * weight_ref[s]
        dst[capacity] = head_ref[p]

    def copy(p, origin):
        return pltpu.make_async_remote_copy(
            src_ref=send_ref.at[p],
            dst_ref=recv_ref.at[origin],
            send_sem=send_sem.at[p],
            recv_sem=recv_sem.at[origin],
            device_id=partner_of(p, width_y),
            device_id_type=pl.DeviceIdType.MESH,
        )

    def give(o, _):
        p = lax.rem(me + o, devices)
        fill(send_ref.at[p], p)
        copy(p, me).start()
        return _

    lax.fori_loop(1, devices, give, 0)
    fill(recv_ref.at[me], me)
    rim.turn()

    gauges = grow_ref.shape[1]
    row_hit = lax.broadcasted_iota(jnp.int32, (high, gauges), 0) == grow_ref[...]
    col_hit = lax.broadcasted_iota(jnp.int32, (wide, gauges), 0) == gcol_ref[...]
    col_hot = col_hit.astype(jnp.float32).astype(jnp.bfloat16)

    def placed(value):
        hot = jnp.where(row_hit, value, 0.0).astype(jnp.bfloat16)
        return lax.dot_general(
            hot, col_hot, (((1,), (1,)), ((), ())), preferred_element_type=jnp.float32
        )

    for q in range(gauge_ref.shape[0]):
        value = value_ref[pl.ds(q, 1), :]
        top = value.astype(jnp.bfloat16).astype(jnp.float32)
        mid = (value - top).astype(jnp.bfloat16).astype(jnp.float32)
        gauge_ref[q] = placed(top) + placed(mid) + placed(value - top - mid)

    rim.end()

    def take(o, _):
        p = lax.rem(me + o, devices)
        copy(me, p).wait_recv()
        return _

    def gone(o, _):
        copy(lax.rem(me + o, devices), me).wait_send()
        return _

    lax.fori_loop(1, devices, take, 0)
    lax.fori_loop(1, devices, gone, 0)


def source_kernel(
    block_ref,
    recv_ref,
    wet_ref,
    ext_ref,
    tile_ref,
    out_buf,
    in_buf,
    rim_send,
    rim_recv,
    *,
    halo,
):
    rows, cols = wet_ref.shape
    slots = block_ref.shape[1]
    count = rows * cols // (SUBL * LANES)
    rim = Rim(ext_ref, out_buf, in_buf, rim_send, rim_recv, rows, cols, halo)
    rim.greet()
    hit = lax.broadcasted_iota(jnp.int32, (count, slots), 0) == block_ref[...]
    hot = hit.astype(jnp.float32).astype(jnp.bfloat16)
    for i in range(SUBL):
        part = recv_ref[pl.ds(i, slots, stride=SUBL), :]
        top = part.astype(jnp.bfloat16)
        rest = (part - top.astype(jnp.float32)).astype(jnp.bfloat16)
        both = jnp.dot(
            hot, jnp.concatenate([top, rest], axis=1), preferred_element_type=jnp.float32
        )
        tile_ref[pl.ds(i, count, stride=SUBL), :] = both[:, :LANES] + both[:, LANES:]
    for c in range(cols // LANES):
        lanes = slice(c * LANES, (c + 1) * LANES)
        ext_ref[0, halo : halo + rows, lanes] = tile_ref[c * rows : (c + 1) * rows, :] * wet_ref[
            :, lanes
        ].astype(jnp.float32)
    rim.pack_columns()
    rim.start(0)
    rim.start(1)
    rim.turn()
    rim.end()


def return_kernel(told_ref, heard_ref, send_sem, recv_sem):
    width_y = lax.axis_size("gy")
    devices = lax.axis_size("gx") * width_y
    me = lax.axis_index("gx") * width_y + lax.axis_index("gy")
    greet_all(me, devices, width_y)

    def copy(p, origin):
        return pltpu.make_async_remote_copy(
            src_ref=told_ref.at[p],
            dst_ref=heard_ref.at[origin],
            send_sem=send_sem.at[p],
            recv_sem=recv_sem.at[origin],
            device_id=partner_of(p, width_y),
            device_id_type=pl.DeviceIdType.MESH,
        )

    def give(o, _):
        copy(lax.rem(me + o, devices), me).start()
        return _

    def take(o, _):
        copy(me, lax.rem(me + o, devices)).wait_recv()
        return _

    def gone(o, _):
        copy(lax.rem(me + o, devices), me).wait_send()
        return _

    lax.fori_loop(1, devices, give, 0)
    heard_ref[me] = told_ref[me]
    lax.fori_loop(1, devices, take, 0)
    lax.fori_loop(1, devices, gone, 0)


def steps_kernel(
    blocks_ref,
    grow_ref,
    gcol_ref,
    start_ref,
    static_ref,
    gauge_ref,
    recv_ref,
    final_ref,
    adjoint_ref,
    slot_ref,
    read_ref,
    face_ref,
    surf_ref,
    flux_ref,
    coef_ref,
    lam_ref,
    pick_ref,
    *,
    steps,
    halo,
    capacity,
):
    high, wide = start_ref.shape
    rows, cols = final_ref.shape
    tall = 2 * SUBL if high % (2 * SUBL) == 0 else SUBL
    strips = high // tall
    per_row = cols // LANES
    line = lax.broadcasted_iota(jnp.int32, (tall, wide), 0)

    def at(i):
        return pl.ds(pl.multiple_of(i * tall, tall), tall)

    def after(i):
        return at(jnp.minimum(i + 1, strips - 1))

    def east(x):
        return pltpu.roll(x, wide - 1, 1)

    def west(x):
        return pltpu.roll(x, 1, 1)

    def south(x, below):
        return jnp.where(line == tall - 1, pltpu.roll(below, tall - 1, 0), pltpu.roll(x, tall - 1, 0))

    def north(x, above):
        return jnp.where(line == 0, pltpu.roll(above, 1, 0), pltpu.roll(x, 1, 0))

    zero = jnp.zeros((tall, wide), jnp.float32)

    def prepare(i, _):
        here, below = at(i), after(i)
        depth, wet, fric = (static_ref[n, here, :] for n in range(3))
        depth_b, wet_b, fric_b = (static_ref[n, below, :] for n in range(3))
        face_ref[0, here, :] = 0.5 * (depth + east(depth))
        face_ref[1, here, :] = wet * east(wet)
        face_ref[2, here, :] = 0.5 * (fric + east(fric))
        face_ref[3, here, :] = 0.5 * (depth + south(depth, depth_b))
        face_ref[4, here, :] = wet * south(wet, wet_b)
        face_ref[5, here, :] = 0.5 * (fric + south(fric, fric_b))
        return _

    lax.fori_loop(0, strips, prepare, 0)

    def face(flux, here, there, depth, wet, rough):
        raw = depth + 0.5 * (here + there)
        total = jnp.maximum(raw, min_depth)
        slope = there - here
        pushed = flux - wave_gain * total * slope
        square = pushed * pushed
        inv_speed = lax.rsqrt(square + speed_floor)
        speed = (square + speed_floor) * inv_speed
        logd = jnp.log(total)
        drag = rough * jnp.exp(logd * (-7.0 / 3.0))
        inv_depth = jnp.exp(-logd)
        ds = drag * speed
        inv = pl.reciprocal(1.0 + ds, approx=True)
        inv = inv * (2.0 - (1.0 + ds) * inv)
        wi = wet * inv
        out = wi * pushed
        d_push = wi * (1.0 - drag * square * inv_speed * inv)
        d_total = (7.0 / 3.0) * out * ds * inv * inv_depth - wave_gain * slope * d_push
        half = jnp.where(raw > min_depth, 0.5, jnp.where(raw == min_depth, 0.25, 0.0))
        both = half * d_total
        apart = wave_gain * total * d_push
        return out, d_push, apart + both, both - apart

    for k in range(steps):
        old = start_ref if k == 0 else surf_ref.at[k - 1]

        def forward(i, carry, k=k, old=old):
            cur, flux_above = carry
            here = at(i)
            nxt = old[after(i), :]
            fe = zero if k == 0 else flux_ref[0, here, :]
            fs = zero if k == 0 else flux_ref[1, here, :]
            ne, ae, xe, ye = face(
                fe, cur, east(cur), face_ref[0, here, :], face_ref[1, here, :], face_ref[2, here, :]
            )
            if k:
                coef_ref[k, 0, here, :] = ae
            coef_ref[k, 1, here, :] = xe
            coef_ref[k, 2, here, :] = ye
            ns, a_s, xs, ys = face(
                fs, cur, south(cur, nxt), face_ref[3, here, :], face_ref[4, here, :], face_ref[5, here, :]
            )
            if k:
                coef_ref[k, 3, here, :] = a_s
            coef_ref[k, 4, here, :] = xs
            coef_ref[k, 5, here, :] = ys
            if k < steps - 1:
                flux_ref[0, here, :] = ne
                flux_ref[1, here, :] = ns
            moved = ne - west(ne) + ns - north(ns, flux_above)
            surf_ref[k, here, :] = static_ref[1, here, :] * (cur - mass_gain * moved)
            return nxt, ns

        lax.fori_loop(0, strips, forward, (old[at(0), :], zero))

    final_ref[...] = surf_ref[steps - 1, halo : halo + rows, :cols]
    mine = grow_ref.shape[0]
    lane = lax.broadcasted_iota(jnp.int32, (mine, wide), 1)
    for k in range(steps):
        for g in range(mine):
            pick_ref[pl.ds(g, 1), :] = surf_ref[k, pl.ds(grow_ref[g], 1), :]
        hit = jnp.where(lane == gcol_ref[...], pick_ref[...], 0.0)
        read_ref[k] = jnp.broadcast_to(jnp.sum(hit, axis=1, keepdims=True), read_ref.shape[1:])

    for k in reversed(range(steps)):
        last = k == steps - 1
        src, dst = lam_ref.at[(k + 1) % 2], lam_ref.at[k % 2]

        def seeded(where, k=k, last=last, src=src):
            seed = gauge_ref[0, where, :] * surf_ref[k, where, :] - gauge_ref[1 + k, where, :]
            total = seed if last else src[where, :] + seed
            return static_ref[1, where, :] * total

        def backward(i, carry, k=k, last=last, dst=dst, seeded=seeded):
            cur, above = carry
            here = at(i)
            nxt = seeded(after(i))
            ge = -mass_gain * (cur - east(cur))
            gs = -mass_gain * (cur - south(cur, nxt))
            if not last:
                ge = ge + flux_ref[0, here, :]
                gs = gs + flux_ref[1, here, :]
            if k:
                flux_ref[0, here, :] = ge * coef_ref[k, 0, here, :]
                flux_ref[1, here, :] = gs * coef_ref[k, 3, here, :]
            ve = ge * coef_ref[k, 2, here, :]
            vs = gs * coef_ref[k, 5, here, :]
            dst[here, :] = (
                cur
                + ge * coef_ref[k, 1, here, :]
                + west(ve)
                + gs * coef_ref[k, 4, here, :]
                + north(vs, above)
            )
            return nxt, vs

        lax.fori_loop(0, strips, backward, (seeded(at(0)), zero))

    adjoint_ref[...] = lam_ref[0, halo : halo + rows, :cols]
    lam_ref[1, halo : halo + rows, :cols] = (
        adjoint_ref[...] * static_ref[1, halo : halo + rows, :cols]
    )

    def dots(d, _):
        for j in range(capacity):
            s = d * capacity + j
            b = blocks_ref[s]
            r = pl.multiple_of(b // per_row * SUBL + halo, SUBL)
            c = pl.multiple_of(b % per_row * LANES, LANES)
            prod = lam_ref[1, pl.ds(r, SUBL), pl.ds(c, LANES)] * recv_ref[d, j]
            slot_ref[d, pl.ds(j, 1), :] = jnp.sum(prod, axis=0, keepdims=True)
        return _

    lax.fori_loop(0, recv_ref.shape[0], dots, 0)


def body(
    ocean_depth,
    wet_mask,
    manning,
    fault_slip,
    pattern,
    foot_tile,
    foot_block,
    gauge_row,
    gauge_col,
    observed,
):
    rows, cols = ocean_depth.shape
    steps = observed.shape[0]
    halo = -(-2 * steps // SUBL) * SUBL
    wide = -(-(cols + 2 * halo) // LANES) * LANES
    high = rows + 2 * halo
    width_x = lax.axis_size("gx")
    width_y = lax.axis_size("gy")
    devices = width_x * width_y
    entries = pattern.shape[0]
    per_fault = entries // fault_slip.shape[0]
    capacity = max(2, (2 * entries + devices - 1) // devices)
    per_row = cols // LANES
    f32 = jnp.float32

    target = foot_tile[:, 0]
    order = jnp.arange(entries, dtype=jnp.int32)
    earlier = (target[:, None] == target[None, :]) & (order[:, None] > order[None, :])
    rank = jnp.sum(earlier.astype(jnp.int32), axis=1)
    place = target * (capacity + 1) + rank
    weights = jnp.repeat(fault_slip, per_fault)
    slots = devices * (capacity + 1)
    is_slot = place[:, None] == jnp.arange(slots, dtype=jnp.int32)[None, :]
    slot_row = jnp.sum(jnp.where(is_slot, order[:, None], 0), axis=0)
    slot_weight = jnp.sum(jnp.where(is_slot, weights[:, None], 0.0), axis=0)
    slot_block = jnp.sum(jnp.where(is_slot, foot_block[:, None], 0), axis=0).astype(f32)
    head = jnp.broadcast_to(
        jnp.pad(slot_block.reshape(devices, 1, capacity + 1), ((0, 0), (0, 0), (0, LANES - capacity - 1))),
        (devices, SUBL, LANES),
    )
    here_x, here_y = lax.axis_index("gx"), lax.axis_index("gy")
    local_row = gauge_row - here_x * rows + halo
    local_col = gauge_col - here_y * cols
    local_col = jnp.where(
        (local_col < -halo) | (local_col >= cols + halo), -1, (local_col + wide) % wide
    )
    values = jnp.concatenate([jnp.ones_like(observed[:1]), observed], axis=0)
    mine = gauge_row.shape[0] // devices
    me = here_x * width_y + here_y
    my_row = lax.dynamic_slice_in_dim(local_row, me * mine, mine)
    my_col = lax.dynamic_slice_in_dim(local_col, me * mine, mine)

    vmem = pl.BlockSpec(memory_space=pltpu.VMEM)
    smem = pl.BlockSpec(memory_space=pltpu.SMEM)
    params = pltpu.CompilerParams(vmem_limit_bytes=52 * 1024 * 1024)

    def remote(number):
        return pltpu.CompilerParams(
            vmem_limit_bytes=48 * 1024 * 1024, collective_id=number, has_side_effects=True
        )

    strip = rows * halo // LANES
    four = [pltpu.SemaphoreType.DMA((4,)), pltpu.SemaphoreType.DMA((4,))]
    every = [pltpu.SemaphoreType.DMA((devices,)), pltpu.SemaphoreType.DMA((devices,))]
    recv, statics, gauges = pl.pallas_call(
        partial(spread_kernel, halo=halo, capacity=capacity),
        out_shape=(
            jax.ShapeDtypeStruct((devices, capacity + 1, SUBL, LANES), f32),
            jax.ShapeDtypeStruct((3, high, wide), f32),
            jax.ShapeDtypeStruct((steps + 1, high, wide), f32),
        ),
        in_specs=[smem] * 2 + [vmem] * 8,
        out_specs=(vmem,) * 3,
        scratch_shapes=[
            pltpu.VMEM((devices, capacity + 1, SUBL, LANES), f32),
            pltpu.VMEM((2, 3, strip, LANES), f32),
            pltpu.VMEM((2, 3, strip, LANES), f32),
        ]
        + every
        + four,
        compiler_params=remote(0),
    )(
        slot_row,
        slot_weight,
        pattern,
        head,
        ocean_depth,
        wet_mask,
        manning,
        local_row[None],
        local_col[None],
        values,
    )
    blocks = recv[:, capacity, 0, : capacity + 1].astype(jnp.int32)
    number = blocks % per_row * (rows // SUBL) + blocks // per_row
    number = jnp.where(jnp.arange(capacity + 1)[None, :] < capacity, number, -1)
    start = pl.pallas_call(
        partial(source_kernel, halo=halo),
        out_shape=jax.ShapeDtypeStruct((1, high, wide), f32),
        in_specs=[vmem] * 3,
        out_specs=vmem,
        scratch_shapes=[
            pltpu.VMEM((rows * cols // LANES, LANES), f32),
            pltpu.VMEM((2, 1, strip, LANES), f32),
            pltpu.VMEM((2, 1, strip, LANES), f32),
        ]
        + four,
        compiler_params=remote(1),
    )(number.reshape(1, slots), recv.reshape(slots * SUBL, LANES), wet_mask)[0]
    blocks = blocks[:, :capacity].reshape(-1)
    final_eta, adjoint, per_slot, reads = pl.pallas_call(
        partial(steps_kernel, steps=steps, halo=halo, capacity=capacity),
        out_shape=(
            jax.ShapeDtypeStruct((rows, cols), f32),
            jax.ShapeDtypeStruct((rows, cols), f32),
            jax.ShapeDtypeStruct((devices, capacity, LANES), f32),
            jax.ShapeDtypeStruct((steps, mine, LANES), f32),
        ),
        in_specs=[smem, smem, vmem, vmem, vmem, vmem, vmem],
        out_specs=(vmem, vmem, vmem, vmem),
        scratch_shapes=[
            pltpu.VMEM((6, high, wide), f32),
            pltpu.VMEM((steps, high, wide), f32),
            pltpu.VMEM((2, high, wide), f32),
            pltpu.VMEM((steps, 6, high, wide), f32),
            pltpu.VMEM((2, high, wide), f32),
            pltpu.VMEM((mine, wide), f32),
        ],
        compiler_params=params,
    )(blocks, my_row, my_col[:, None], start, statics, gauges, recv)
    told = jnp.concatenate(
        [
            jnp.sum(per_slot, axis=2),
            jnp.zeros((devices, 1), f32),
            jnp.broadcast_to(reads[:, :, 0].reshape(1, -1), (devices, steps * mine)),
        ],
        axis=1,
    )
    told = jnp.pad(told, ((0, 0), (0, -told.shape[1] % LANES)))
    heard = pl.pallas_call(
        return_kernel,
        out_shape=jax.ShapeDtypeStruct((devices, 1, told.shape[1]), f32),
        in_specs=[vmem],
        out_specs=vmem,
        scratch_shapes=every,
        compiler_params=remote(2),
    )(told[:, None, :])[:, 0]
    readings = heard[:, capacity + 1 : capacity + 1 + steps * mine].reshape(devices, steps, mine)
    readings = readings.transpose(1, 0, 2).reshape(steps, devices * mine)
    heard = heard[:, : capacity + 1].reshape(1, -1)
    per_entry = jnp.sum(jnp.where(is_slot, heard, 0.0), axis=1)
    grad_slip = jnp.sum(per_entry.reshape(-1, per_fault), axis=1) / fault_slip
    return (final_eta, readings, adjoint, grad_slip)


def solution(mesh):
    placed = (
        P("gx", "gy"),
        P("gx", "gy"),
        P("gx", "gy"),
        P(("gx", "gy")),
        P(("gx", "gy"), None, None),
        P(("gx", "gy"), None),
        P(("gx", "gy")),
        P(),
        P(),
        P(),
    )
    return jax.shard_map(
        body,
        mesh=mesh,
        in_specs=placed,
        out_specs=(P("gx", "gy"), P(), P("gx", "gy"), P(("gx", "gy"))),
        check_vma=False,
    )
```

```python
from functools import partial

import jax
import jax.numpy as jnp
from jax import lax
from jax.experimental import pallas as pl
from jax.experimental.pallas import tpu as pltpu
from jax.sharding import PartitionSpec as P

wave_gain = 0.2
mass_gain = 0.2
min_depth = 0.25
speed_floor = 0.01
LANES = 128
SUBL = 8
LIMIT = 60 * 1024 * 1024


def partner_of(number, width_y):
    return {"gx": number // width_y, "gy": lax.rem(number, width_y)}


def greet_all(me, devices, width_y):
    barrier = pltpu.get_barrier_semaphore()

    def greet(o, _):
        other = partner_of(lax.rem(me + o, devices), width_y)
        pl.semaphore_signal(barrier, inc=1, device_id=other, device_id_type=pl.DeviceIdType.MESH)
        return _

    lax.fori_loop(1, devices, greet, 0)
    pl.semaphore_wait(barrier, devices - 1)


def pack(x, first, halo):
    parts = LANES // halo
    per = x.shape[0] // parts
    group = lax.broadcasted_iota(jnp.int32, (per, LANES), 1) // halo
    out = jnp.zeros((per, LANES), x.dtype)
    for c in range(parts):
        by = (c * halo - first) % LANES
        part = x[c * per : (c + 1) * per]
        out = jnp.where(group == c, pltpu.roll(part, by, 1) if by else part, out)
    return out


def unpack(x, first, halo):
    lane = lax.broadcasted_iota(jnp.int32, x.shape, 1)
    inside = (lane >= first) & (lane < first + halo)
    out = []
    for c in range(LANES // halo):
        by = (first - c * halo) % LANES
        out.append(jnp.where(inside, pltpu.roll(x, by, 1) if by else x, 0.0))
    return jnp.concatenate(out, axis=0)


class Rim:
    def __init__(self, ext_ref, out_buf, in_buf, send_sem, recv_sem, rows, cols, halo):
        self.ext, self.out, self.inn = ext_ref, out_buf, in_buf
        self.rows, self.cols, self.halo = rows, cols, halo
        x, y = lax.axis_index("gx"), lax.axis_index("gy")
        self.has = (
            y > 0,
            y < lax.axis_size("gy") - 1,
            x > 0,
            x < lax.axis_size("gx") - 1,
        )
        self.to = ({"gy": y - 1}, {"gy": y + 1}, {"gx": x - 1}, {"gx": x + 1})
        low, end = halo, halo + rows
        ends = (
            (out_buf.at[0], in_buf.at[1]),
            (out_buf.at[1], in_buf.at[0]),
            (ext_ref.at[:, low : low + halo, :], ext_ref.at[:, end : end + halo, :]),
            (ext_ref.at[:, end - halo : end, :], ext_ref.at[:, 0:halo, :]),
        )
        back = (1, 0, 3, 2)
        self.copies = [
            pltpu.make_async_remote_copy(
                src_ref=ends[d][0],
                dst_ref=ends[d][1],
                send_sem=send_sem.at[d],
                recv_sem=recv_sem.at[back[d]],
                device_id=self.to[d],
                device_id_type=pl.DeviceIdType.MESH,
            )
            for d in range(4)
        ]
        self.back = back

    def greet(self):
        barrier = pltpu.get_barrier_semaphore()
        for has, to in zip(self.has, self.to):

            @pl.when(has)
            def _(to=to):
                pl.semaphore_signal(
                    barrier, inc=1, device_id=to, device_id_type=pl.DeviceIdType.MESH
                )

        pl.semaphore_wait(barrier, sum(has.astype(jnp.int32) for has in self.has))

    def pack_columns(self):
        inner = slice(self.halo, self.halo + self.rows)
        for f in range(self.ext.shape[0]):
            self.out[0, f] = pack(self.ext[f, inner, :LANES], 0, self.halo)
            self.out[1, f] = pack(
                self.ext[f, inner, self.cols - LANES : self.cols], LANES - self.halo, self.halo
            )

    def start(self, d):
        @pl.when(self.has[d])
        def _():
            self.copies[d].start()

    def finish(self, d):
        @pl.when(self.has[d])
        def _():
            self.copies[self.back[d]].wait_recv()

        @pl.when(jnp.logical_not(self.has[d]))
        def _():
            if d < 2:
                self.inn[d] = jnp.zeros(self.inn.shape[1:], jnp.float32)
            else:
                at = 0 if d == 2 else self.halo + self.rows
                self.ext[:, at : at + self.halo, :] = jnp.zeros(
                    (self.ext.shape[0], self.halo, self.ext.shape[2]), jnp.float32
                )

    def turn(self):
        self.finish(0)
        self.finish(1)
        inner = slice(self.halo, self.halo + self.rows)
        for f in range(self.ext.shape[0]):
            self.ext[f, inner, self.cols :] = unpack(self.inn[1, f], 0, self.halo) + unpack(
                self.inn[0, f], LANES - self.halo, self.halo
            )
        self.start(2)
        self.start(3)

    def end(self):
        self.finish(2)
        self.finish(3)
        for d in range(4):

            @pl.when(self.has[d])
            def _(d=d):
                self.copies[d].wait_send()


def spread_kernel(
    row_ref,
    weight_ref,
    pattern_ref,
    head_ref,
    depth_ref,
    wet_ref,
    fric_ref,
    grow_ref,
    gcol_ref,
    value_ref,
    recv_ref,
    heads_ref,
    static_ref,
    gauge_ref,
    send_ref,
    out_buf,
    in_buf,
    send_sem,
    recv_sem,
    head_send,
    head_recv,
    rim_send,
    rim_recv,
    *,
    halo,
    capacity,
):
    rows, cols = depth_ref.shape
    high, wide = static_ref.shape[1:]
    width_y = lax.axis_size("gy")
    devices = lax.axis_size("gx") * width_y
    me = lax.axis_index("gx") * width_y + lax.axis_index("gy")
    rim = Rim(static_ref, out_buf, in_buf, rim_send, rim_recv, rows, cols, halo)
    for f, ref in enumerate((depth_ref, wet_ref, fric_ref)):
        static_ref[f, halo : halo + rows, :cols] = ref[...].astype(jnp.float32)
    greet_all(me, devices, width_y)

    def fill(dst, p):
        for j in range(capacity):
            s = p * capacity + j
            dst[j] = pattern_ref[row_ref[s]] * weight_ref[s]

    def copy(p, origin):
        return pltpu.make_async_remote_copy(
            src_ref=send_ref.at[p],
            dst_ref=recv_ref.at[origin],
            send_sem=send_sem.at[p],
            recv_sem=recv_sem.at[origin],
            device_id=partner_of(p, width_y),
            device_id_type=pl.DeviceIdType.MESH,
        )

    def copy_head(p, origin):
        return pltpu.make_async_remote_copy(
            src_ref=head_ref.at[p],
            dst_ref=heads_ref.at[origin],
            send_sem=head_send.at[p],
            recv_sem=head_recv.at[origin],
            device_id=partner_of(p, width_y),
            device_id_type=pl.DeviceIdType.MESH,
        )

    def give(o, _):
        p = lax.rem(me + o, devices)
        fill(send_ref.at[p], p)
        copy(p, me).start()
        copy_head(p, me).start()
        return _

    early = min(5, devices)
    lax.fori_loop(1, early, give, 0)
    rim.pack_columns()
    rim.start(0)
    rim.start(1)
    lax.fori_loop(early, devices, give, 0)
    fill(recv_ref.at[me], me)
    heads_ref[me] = head_ref[me]
    rim.turn()

    gauges = grow_ref.shape[1]
    row_hit = lax.broadcasted_iota(jnp.int32, (high, gauges), 0) == grow_ref[...]
    col_hit = lax.broadcasted_iota(jnp.int32, (wide, gauges), 0) == gcol_ref[...]
    col_hot = col_hit.astype(jnp.float32).astype(jnp.bfloat16)

    def placed(value):
        hot = jnp.where(row_hit, value, 0.0).astype(jnp.bfloat16)
        return lax.dot_general(
            hot, col_hot, (((1,), (1,)), ((), ())), preferred_element_type=jnp.float32
        )

    for q in range(gauge_ref.shape[0]):
        value = value_ref[pl.ds(q, 1), :]
        top = value.astype(jnp.bfloat16).astype(jnp.float32)
        mid = (value - top).astype(jnp.bfloat16).astype(jnp.float32)
        gauge_ref[q] = placed(top) + placed(mid) + placed(value - top - mid)

    rim.end()

    def take(o, _):
        p = lax.rem(me + o, devices)
        copy(me, p).wait_recv()
        copy_head(me, p).wait_recv()
        return _

    def gone(o, _):
        p = lax.rem(me + o, devices)
        copy(p, me).wait_send()
        copy_head(p, me).wait_send()
        return _

    lax.fori_loop(1, devices, take, 0)
    lax.fori_loop(1, devices, gone, 0)


def source_kernel(
    block_ref,
    recv_ref,
    wet_ref,
    ext_ref,
    tile_ref,
    out_buf,
    in_buf,
    rim_send,
    rim_recv,
    *,
    halo,
):
    rows, cols = wet_ref.shape
    slots = block_ref.shape[1]
    count = rows * cols // (SUBL * LANES)
    rim = Rim(ext_ref, out_buf, in_buf, rim_send, rim_recv, rows, cols, halo)
    rim.greet()
    hit = lax.broadcasted_iota(jnp.int32, (count, slots), 0) == block_ref[...]
    hot = hit.astype(jnp.float32).astype(jnp.bfloat16)
    for i in range(SUBL):
        part = recv_ref[pl.ds(i, slots, stride=SUBL), :]
        top = part.astype(jnp.bfloat16)
        rest = (part - top.astype(jnp.float32)).astype(jnp.bfloat16)
        both = jnp.dot(
            hot, jnp.concatenate([top, rest], axis=1), preferred_element_type=jnp.float32
        )
        tile_ref[pl.ds(i, count, stride=SUBL), :] = both[:, :LANES] + both[:, LANES:]
    for c in range(cols // LANES):
        lanes = slice(c * LANES, (c + 1) * LANES)
        ext_ref[0, halo : halo + rows, lanes] = tile_ref[c * rows : (c + 1) * rows, :] * wet_ref[
            :, lanes
        ].astype(jnp.float32)
    rim.pack_columns()
    rim.start(0)
    rim.start(1)
    rim.turn()
    rim.end()


def return_kernel(told_ref, heard_ref, send_sem, recv_sem):
    width_y = lax.axis_size("gy")
    devices = lax.axis_size("gx") * width_y
    me = lax.axis_index("gx") * width_y + lax.axis_index("gy")
    greet_all(me, devices, width_y)

    def copy(p, origin):
        return pltpu.make_async_remote_copy(
            src_ref=told_ref.at[p],
            dst_ref=heard_ref.at[origin],
            send_sem=send_sem.at[p],
            recv_sem=recv_sem.at[origin],
            device_id=partner_of(p, width_y),
            device_id_type=pl.DeviceIdType.MESH,
        )

    def give(o, _):
        copy(lax.rem(me + o, devices), me).start()
        return _

    def take(o, _):
        copy(me, lax.rem(me + o, devices)).wait_recv()
        return _

    def gone(o, _):
        copy(lax.rem(me + o, devices), me).wait_send()
        return _

    lax.fori_loop(1, devices, give, 0)
    heard_ref[me] = told_ref[me]
    lax.fori_loop(1, devices, take, 0)
    lax.fori_loop(1, devices, gone, 0)


def steps_kernel(
    blocks_ref,
    grow_ref,
    gcol_ref,
    start_ref,
    static_ref,
    gauge_ref,
    recv_ref,
    final_ref,
    adjoint_ref,
    slot_ref,
    read_ref,
    face_ref,
    surf_ref,
    flux_ref,
    coef_ref,
    lam_ref,
    pick_ref,
    *,
    steps,
    halo,
    capacity,
):
    high, wide = start_ref.shape
    rows, cols = final_ref.shape
    tall = 2 * SUBL if high % (2 * SUBL) == 0 else SUBL
    strips = high // tall
    per_row = cols // LANES
    line = lax.broadcasted_iota(jnp.int32, (tall, wide), 0)

    def at(i):
        return pl.ds(pl.multiple_of(i * tall, tall), tall)

    def after(i):
        return at(jnp.minimum(i + 1, strips - 1))

    def east(x):
        return pltpu.roll(x, wide - 1, 1)

    def west(x):
        return pltpu.roll(x, 1, 1)

    def south(x, below):
        return jnp.where(line == tall - 1, pltpu.roll(below, tall - 1, 0), pltpu.roll(x, tall - 1, 0))

    def north(x, above):
        return jnp.where(line == 0, pltpu.roll(above, 1, 0), pltpu.roll(x, 1, 0))

    zero = jnp.zeros((tall, wide), jnp.float32)

    def prepare(i, _):
        here, below = at(i), after(i)
        depth, wet, fric = (static_ref[n, here, :] for n in range(3))
        depth_b, wet_b, fric_b = (static_ref[n, below, :] for n in range(3))
        face_ref[0, here, :] = 0.5 * (depth + east(depth))
        face_ref[1, here, :] = wet * east(wet)
        face_ref[2, here, :] = 0.5 * (fric + east(fric))
        face_ref[3, here, :] = 0.5 * (depth + south(depth, depth_b))
        face_ref[4, here, :] = wet * south(wet, wet_b)
        face_ref[5, here, :] = 0.5 * (fric + south(fric, fric_b))
        return _

    lax.fori_loop(0, strips, prepare, 0)

    def sweep(work, carry):
        carry = lax.fori_loop(0, strips // 2, lambda j, c: work(2 * j + 1, work(2 * j, c)), carry)
        if strips % 2:
            work(strips - 1, carry)

    def face(flux, here, there, depth, wet, rough):
        raw = depth + 0.5 * (here + there)
        total = jnp.maximum(raw, min_depth)
        slope = there - here
        pushed = flux - wave_gain * total * slope
        square = pushed * pushed
        inv_speed = lax.rsqrt(square + speed_floor)
        speed = (square + speed_floor) * inv_speed
        logd = jnp.log(total)
        drag = rough * jnp.exp(logd * (-7.0 / 3.0))
        inv_depth = jnp.exp(-logd)
        ds = drag * speed
        inv = pl.reciprocal(1.0 + ds, approx=True)
        inv = inv * (2.0 - (1.0 + ds) * inv)
        wi = wet * inv
        out = wi * pushed
        d_push = wi * (1.0 - drag * square * inv_speed * inv)
        d_total = (7.0 / 3.0) * out * ds * inv * inv_depth - wave_gain * slope * d_push
        half = jnp.where(raw > min_depth, 0.5, jnp.where(raw == min_depth, 0.25, 0.0))
        both = half * d_total
        apart = wave_gain * total * d_push
        return out, d_push, apart + both, both - apart

    for k in range(steps):
        old = start_ref if k == 0 else surf_ref.at[k - 1]

        def forward(i, carry, k=k, old=old):
            cur, flux_above = carry
            here = at(i)
            nxt = old[after(i), :]
            fe = zero if k == 0 else flux_ref[0, here, :]
            fs = zero if k == 0 else flux_ref[1, here, :]
            ne, ae, xe, ye = face(
                fe, cur, east(cur), face_ref[0, here, :], face_ref[1, here, :], face_ref[2, here, :]
            )
            if k:
                coef_ref[k, 0, here, :] = ae
            coef_ref[k, 1, here, :] = xe
            coef_ref[k, 2, here, :] = ye
            ns, a_s, xs, ys = face(
                fs, cur, south(cur, nxt), face_ref[3, here, :], face_ref[4, here, :], face_ref[5, here, :]
            )
            if k:
                coef_ref[k, 3, here, :] = a_s
            coef_ref[k, 4, here, :] = xs
            coef_ref[k, 5, here, :] = ys
            if k < steps - 1:
                flux_ref[0, here, :] = ne
                flux_ref[1, here, :] = ns
            moved = ne - west(ne) + ns - north(ns, flux_above)
            surf_ref[k, here, :] = static_ref[1, here, :] * (cur - mass_gain * moved)
            return nxt, ns

        sweep(forward, (old[at(0), :], zero))

    final_ref[...] = surf_ref[steps - 1, halo : halo + rows, :cols]
    mine = grow_ref.shape[0]
    lane = lax.broadcasted_iota(jnp.int32, (mine, wide), 1)
    for k in range(steps):
        for g in range(mine):
            pick_ref[pl.ds(g, 1), :] = surf_ref[k, pl.ds(grow_ref[g], 1), :]
        hit = jnp.where(lane == gcol_ref[...], pick_ref[...], 0.0)
        read_ref[k] = jnp.broadcast_to(jnp.sum(hit, axis=1, keepdims=True), read_ref.shape[1:])

    for k in reversed(range(steps)):
        last = k == steps - 1
        src, dst = lam_ref.at[(k + 1) % 2], lam_ref.at[k % 2]

        def seeded(where, k=k, last=last, src=src):
            seed = gauge_ref[0, where, :] * surf_ref[k, where, :] - gauge_ref[1 + k, where, :]
            total = seed if last else src[where, :] + seed
            return static_ref[1, where, :] * total

        def backward(i, carry, k=k, last=last, dst=dst, seeded=seeded):
            cur, above = carry
            here = at(i)
            nxt = seeded(after(i))
            ge = -mass_gain * (cur - east(cur))
            gs = -mass_gain * (cur - south(cur, nxt))
            if not last:
                ge = ge + flux_ref[0, here, :]
                gs = gs + flux_ref[1, here, :]
            if k:
                flux_ref[0, here, :] = ge * coef_ref[k, 0, here, :]
                flux_ref[1, here, :] = gs * coef_ref[k, 3, here, :]
            ve = ge * coef_ref[k, 2, here, :]
            vs = gs * coef_ref[k, 5, here, :]
            dst[here, :] = (
                cur
                + ge * coef_ref[k, 1, here, :]
                + west(ve)
                + gs * coef_ref[k, 4, here, :]
                + north(vs, above)
            )
            return nxt, vs

        sweep(backward, (seeded(at(0)), zero))

    adjoint_ref[...] = lam_ref[0, halo : halo + rows, :cols]
    lam_ref[1, halo : halo + rows, :cols] = (
        adjoint_ref[...] * static_ref[1, halo : halo + rows, :cols]
    )

    def dots(d, _):
        for j in range(capacity):
            s = d * capacity + j
            b = blocks_ref[s]
            r = pl.multiple_of(b // per_row * SUBL + halo, SUBL)
            c = pl.multiple_of(b % per_row * LANES, LANES)
            prod = lam_ref[1, pl.ds(r, SUBL), pl.ds(c, LANES)] * recv_ref[d, j]
            slot_ref[d, pl.ds(j, 1), :] = jnp.sum(prod, axis=0, keepdims=True)
        return _

    lax.fori_loop(0, recv_ref.shape[0], dots, 0)


def body(
    ocean_depth,
    wet_mask,
    manning,
    fault_slip,
    pattern,
    foot_tile,
    foot_block,
    gauge_row,
    gauge_col,
    observed,
):
    rows, cols = ocean_depth.shape
    steps = observed.shape[0]
    halo = -(-2 * steps // SUBL) * SUBL
    wide = -(-(cols + 2 * halo) // LANES) * LANES
    high = rows + 2 * halo
    width_x = lax.axis_size("gx")
    width_y = lax.axis_size("gy")
    devices = width_x * width_y
    entries = pattern.shape[0]
    per_fault = entries // fault_slip.shape[0]
    capacity = max(2, (2 * entries + devices - 1) // devices)
    per_row = cols // LANES
    f32 = jnp.float32

    target = foot_tile[:, 0]
    order = jnp.arange(entries, dtype=jnp.int32)
    earlier = (target[:, None] == target[None, :]) & (order[:, None] > order[None, :])
    rank = jnp.sum(earlier.astype(jnp.int32), axis=1)
    place = target * capacity + rank
    weights = jnp.repeat(fault_slip, per_fault)
    slots = devices * capacity
    is_slot = place[:, None] == jnp.arange(slots, dtype=jnp.int32)[None, :]
    slot_row = jnp.sum(jnp.where(is_slot, order[:, None], 0), axis=0)
    slot_weight = jnp.sum(jnp.where(is_slot, weights[:, None], 0.0), axis=0)
    slot_block = jnp.sum(jnp.where(is_slot, foot_block[:, None], 0), axis=0).astype(f32)
    head = jnp.pad(slot_block.reshape(devices, 1, capacity), ((0, 0), (0, 0), (0, LANES - capacity)))
    here_x, here_y = lax.axis_index("gx"), lax.axis_index("gy")
    local_row = gauge_row - here_x * rows + halo
    local_col = gauge_col - here_y * cols
    local_col = jnp.where(
        (local_col < -halo) | (local_col >= cols + halo), -1, (local_col + wide) % wide
    )
    values = jnp.concatenate([jnp.ones_like(observed[:1]), observed], axis=0)
    mine = gauge_row.shape[0] // devices
    me = here_x * width_y + here_y
    my_row = lax.dynamic_slice_in_dim(local_row, me * mine, mine)
    my_col = lax.dynamic_slice_in_dim(local_col, me * mine, mine)

    vmem = pl.BlockSpec(memory_space=pltpu.VMEM)
    smem = pl.BlockSpec(memory_space=pltpu.SMEM)
    params = pltpu.CompilerParams(vmem_limit_bytes=LIMIT)

    def remote(number):
        return pltpu.CompilerParams(
            vmem_limit_bytes=LIMIT, collective_id=number, has_side_effects=True
        )

    strip = rows * halo // LANES
    four = [pltpu.SemaphoreType.DMA((4,)), pltpu.SemaphoreType.DMA((4,))]
    every = [pltpu.SemaphoreType.DMA((devices,)), pltpu.SemaphoreType.DMA((devices,))]
    recv, heads, statics, gauges = pl.pallas_call(
        partial(spread_kernel, halo=halo, capacity=capacity),
        out_shape=(
            jax.ShapeDtypeStruct((devices, capacity, SUBL, LANES), f32),
            jax.ShapeDtypeStruct((devices, 1, LANES), f32),
            jax.ShapeDtypeStruct((3, high, wide), f32),
            jax.ShapeDtypeStruct((steps + 1, high, wide), f32),
        ),
        in_specs=[smem] * 2 + [vmem] * 8,
        out_specs=(vmem,) * 4,
        scratch_shapes=[
            pltpu.VMEM((devices, capacity, SUBL, LANES), f32),
            pltpu.VMEM((2, 3, strip, LANES), f32),
            pltpu.VMEM((2, 3, strip, LANES), f32),
        ]
        + every * 2
        + four,
        compiler_params=remote(0),
    )(
        slot_row,
        slot_weight,
        pattern,
        head,
        ocean_depth,
        wet_mask,
        manning,
        local_row[None],
        local_col[None],
        values,
    )
    blocks = heads[:, 0, :capacity].astype(jnp.int32)
    number = blocks % per_row * (rows // SUBL) + blocks // per_row
    start = pl.pallas_call(
        partial(source_kernel, halo=halo),
        out_shape=jax.ShapeDtypeStruct((1, high, wide), f32),
        in_specs=[vmem] * 3,
        out_specs=vmem,
        scratch_shapes=[
            pltpu.VMEM((rows * cols // LANES, LANES), f32),
            pltpu.VMEM((2, 1, strip, LANES), f32),
            pltpu.VMEM((2, 1, strip, LANES), f32),
        ]
        + four,
        compiler_params=remote(1),
    )(number.reshape(1, slots), recv.reshape(slots * SUBL, LANES), wet_mask)[0]
    blocks = blocks.reshape(-1)
    final_eta, adjoint, per_slot, reads = pl.pallas_call(
        partial(steps_kernel, steps=steps, halo=halo, capacity=capacity),
        out_shape=(
            jax.ShapeDtypeStruct((rows, cols), f32),
            jax.ShapeDtypeStruct((rows, cols), f32),
            jax.ShapeDtypeStruct((devices, capacity, LANES), f32),
            jax.ShapeDtypeStruct((steps, mine, LANES), f32),
        ),
        in_specs=[smem, smem, vmem, vmem, vmem, vmem, vmem],
        out_specs=(vmem, vmem, vmem, vmem),
        scratch_shapes=[
            pltpu.VMEM((6, high, wide), f32),
            pltpu.VMEM((steps, high, wide), f32),
            pltpu.VMEM((2, high, wide), f32),
            pltpu.VMEM((steps, 6, high, wide), f32),
            pltpu.VMEM((2, high, wide), f32),
            pltpu.VMEM((mine, wide), f32),
        ],
        compiler_params=params,
    )(blocks, my_row, my_col[:, None], start, statics, gauges, recv)
    told = jnp.concatenate(
        [
            jnp.sum(per_slot, axis=2),
            jnp.broadcast_to(reads[:, :, 0].reshape(1, -1), (devices, steps * mine)),
        ],
        axis=1,
    )
    told = jnp.pad(told, ((0, 0), (0, -told.shape[1] % LANES)))
    heard = pl.pallas_call(
        return_kernel,
        out_shape=jax.ShapeDtypeStruct((devices, 1, told.shape[1]), f32),
        in_specs=[vmem],
        out_specs=vmem,
        scratch_shapes=every,
        compiler_params=remote(2),
    )(told[:, None, :])[:, 0]
    readings = heard[:, capacity : capacity + steps * mine].reshape(devices, steps, mine)
    readings = readings.transpose(1, 0, 2).reshape(steps, devices * mine)
    heard = heard[:, :capacity].reshape(1, -1)
    per_entry = jnp.sum(jnp.where(is_slot, heard, 0.0), axis=1)
    grad_slip = jnp.sum(per_entry.reshape(-1, per_fault), axis=1) / fault_slip
    return (final_eta, readings, adjoint, grad_slip)


def solution(mesh):
    placed = (
        P("gx", "gy"),
        P("gx", "gy"),
        P("gx", "gy"),
        P(("gx", "gy")),
        P(("gx", "gy"), None, None),
        P(("gx", "gy"), None),
        P(("gx", "gy")),
        P(),
        P(),
        P(),
    )
    return jax.shard_map(
        body,
        mesh=mesh,
        in_specs=placed,
        out_specs=(P("gx", "gy"), P(), P("gx", "gy"), P(("gx", "gy"))),
        check_vma=False,
    )
```

```python
from functools import partial

import jax
import jax.numpy as jnp
from jax import lax
from jax.experimental import pallas as pl
from jax.experimental.pallas import tpu as pltpu
from jax.sharding import PartitionSpec as P

wave_gain = 0.2
mass_gain = 0.2
min_depth = 0.25
speed_floor = 0.01
LANES = 128
SUBL = 8
LIMIT = 60 * 1024 * 1024


def partner_of(number, width_y):
    return {"gx": number // width_y, "gy": lax.rem(number, width_y)}


def greet_all(me, devices, width_y):
    barrier = pltpu.get_barrier_semaphore()

    def greet(o, _):
        other = partner_of(lax.rem(me + o, devices), width_y)
        pl.semaphore_signal(barrier, inc=1, device_id=other, device_id_type=pl.DeviceIdType.MESH)
        return _

    lax.fori_loop(1, devices, greet, 0)
    pl.semaphore_wait(barrier, devices - 1)


def pack(x, first, halo):
    parts = LANES // halo
    per = x.shape[0] // parts
    group = lax.broadcasted_iota(jnp.int32, (per, LANES), 1) // halo
    out = jnp.zeros((per, LANES), x.dtype)
    for c in range(parts):
        by = (c * halo - first) % LANES
        part = x[c * per : (c + 1) * per]
        out = jnp.where(group == c, pltpu.roll(part, by, 1) if by else part, out)
    return out


def unpack(x, first, halo):
    lane = lax.broadcasted_iota(jnp.int32, x.shape, 1)
    inside = (lane >= first) & (lane < first + halo)
    out = []
    for c in range(LANES // halo):
        by = (first - c * halo) % LANES
        out.append(jnp.where(inside, pltpu.roll(x, by, 1) if by else x, 0.0))
    return jnp.concatenate(out, axis=0)


class Rim:
    def __init__(self, ext_ref, out_buf, in_buf, send_sem, recv_sem, rows, cols, halo):
        self.ext, self.out, self.inn = ext_ref, out_buf, in_buf
        self.rows, self.cols, self.halo = rows, cols, halo
        x, y = lax.axis_index("gx"), lax.axis_index("gy")
        self.has = (
            y > 0,
            y < lax.axis_size("gy") - 1,
            x > 0,
            x < lax.axis_size("gx") - 1,
        )
        self.to = ({"gy": y - 1}, {"gy": y + 1}, {"gx": x - 1}, {"gx": x + 1})
        low, end = halo, halo + rows
        ends = (
            (out_buf.at[0], in_buf.at[1]),
            (out_buf.at[1], in_buf.at[0]),
            (ext_ref.at[:, low : low + halo, :], ext_ref.at[:, end : end + halo, :]),
            (ext_ref.at[:, end - halo : end, :], ext_ref.at[:, 0:halo, :]),
        )
        back = (1, 0, 3, 2)
        self.copies = [
            pltpu.make_async_remote_copy(
                src_ref=ends[d][0],
                dst_ref=ends[d][1],
                send_sem=send_sem.at[d],
                recv_sem=recv_sem.at[back[d]],
                device_id=self.to[d],
                device_id_type=pl.DeviceIdType.MESH,
            )
            for d in range(4)
        ]
        self.back = back

    def greet(self):
        barrier = pltpu.get_barrier_semaphore()
        for has, to in zip(self.has, self.to):

            @pl.when(has)
            def _(to=to):
                pl.semaphore_signal(
                    barrier, inc=1, device_id=to, device_id_type=pl.DeviceIdType.MESH
                )

        pl.semaphore_wait(barrier, sum(has.astype(jnp.int32) for has in self.has))

    def pack_columns(self):
        inner = slice(self.halo, self.halo + self.rows)
        for f in range(self.ext.shape[0]):
            self.out[0, f] = pack(self.ext[f, inner, :LANES], 0, self.halo)
            self.out[1, f] = pack(
                self.ext[f, inner, self.cols - LANES : self.cols], LANES - self.halo, self.halo
            )

    def start(self, d):
        @pl.when(self.has[d])
        def _():
            self.copies[d].start()

    def finish(self, d):
        @pl.when(self.has[d])
        def _():
            self.copies[self.back[d]].wait_recv()

        @pl.when(jnp.logical_not(self.has[d]))
        def _():
            if d < 2:
                self.inn[d] = jnp.zeros(self.inn.shape[1:], jnp.float32)
            else:
                at = 0 if d == 2 else self.halo + self.rows
                self.ext[:, at : at + self.halo, :] = jnp.zeros(
                    (self.ext.shape[0], self.halo, self.ext.shape[2]), jnp.float32
                )

    def turn(self):
        self.finish(0)
        self.finish(1)
        inner = slice(self.halo, self.halo + self.rows)
        for f in range(self.ext.shape[0]):
            self.ext[f, inner, self.cols :] = unpack(self.inn[1, f], 0, self.halo) + unpack(
                self.inn[0, f], LANES - self.halo, self.halo
            )
        self.start(2)
        self.start(3)

    def end(self):
        self.finish(2)
        self.finish(3)
        for d in range(4):

            @pl.when(self.has[d])
            def _(d=d):
                self.copies[d].wait_send()


def spread_kernel(
    row_ref,
    weight_ref,
    pattern_ref,
    head_ref,
    depth_ref,
    wet_ref,
    fric_ref,
    grow_ref,
    gcol_ref,
    value_ref,
    recv_ref,
    heads_ref,
    static_ref,
    gauge_ref,
    send_ref,
    out_buf,
    in_buf,
    send_sem,
    recv_sem,
    head_send,
    head_recv,
    rim_send,
    rim_recv,
    *,
    halo,
    capacity,
):
    rows, cols = depth_ref.shape
    high, wide = static_ref.shape[1:]
    width_y = lax.axis_size("gy")
    devices = lax.axis_size("gx") * width_y
    me = lax.axis_index("gx") * width_y + lax.axis_index("gy")
    rim = Rim(static_ref, out_buf, in_buf, rim_send, rim_recv, rows, cols, halo)
    for f, ref in enumerate((depth_ref, wet_ref, fric_ref)):
        static_ref[f, halo : halo + rows, :cols] = ref[...].astype(jnp.float32)
    greet_all(me, devices, width_y)

    def fill(dst, p):
        for j in range(capacity):
            s = p * capacity + j
            dst[j] = pattern_ref[row_ref[s]] * weight_ref[s]

    def copy(p, origin):
        return pltpu.make_async_remote_copy(
            src_ref=send_ref.at[p],
            dst_ref=recv_ref.at[origin],
            send_sem=send_sem.at[p],
            recv_sem=recv_sem.at[origin],
            device_id=partner_of(p, width_y),
            device_id_type=pl.DeviceIdType.MESH,
        )

    def copy_head(p, origin):
        return pltpu.make_async_remote_copy(
            src_ref=head_ref.at[p],
            dst_ref=heads_ref.at[origin],
            send_sem=head_send.at[p],
            recv_sem=head_recv.at[origin],
            device_id=partner_of(p, width_y),
            device_id_type=pl.DeviceIdType.MESH,
        )

    def give(o, _):
        p = lax.rem(me + o, devices)
        fill(send_ref.at[p], p)
        copy(p, me).start()
        copy_head(p, me).start()
        return _

    early = min(5, devices)
    lax.fori_loop(1, early, give, 0)
    rim.pack_columns()
    rim.start(0)
    rim.start(1)
    lax.fori_loop(early, devices, give, 0)
    fill(recv_ref.at[me], me)
    heads_ref[me] = head_ref[me]
    rim.turn()

    gauges = grow_ref.shape[1]
    row_hit = lax.broadcasted_iota(jnp.int32, (high, gauges), 0) == grow_ref[...]
    col_hit = lax.broadcasted_iota(jnp.int32, (wide, gauges), 0) == gcol_ref[...]
    col_hot = col_hit.astype(jnp.float32).astype(jnp.bfloat16)

    def placed(value):
        hot = jnp.where(row_hit, value, 0.0).astype(jnp.bfloat16)
        return lax.dot_general(
            hot, col_hot, (((1,), (1,)), ((), ())), preferred_element_type=jnp.float32
        )

    for q in range(gauge_ref.shape[0]):
        value = value_ref[pl.ds(q, 1), :]
        top = value.astype(jnp.bfloat16).astype(jnp.float32)
        mid = (value - top).astype(jnp.bfloat16).astype(jnp.float32)
        gauge_ref[q] = placed(top) + placed(mid) + placed(value - top - mid)

    rim.end()

    def take(o, _):
        p = lax.rem(me + o, devices)
        copy(me, p).wait_recv()
        copy_head(me, p).wait_recv()
        return _

    def gone(o, _):
        p = lax.rem(me + o, devices)
        copy(p, me).wait_send()
        copy_head(p, me).wait_send()
        return _

    lax.fori_loop(1, devices, take, 0)
    lax.fori_loop(1, devices, gone, 0)


def source_kernel(
    block_ref,
    recv_ref,
    wet_ref,
    ext_ref,
    tile_ref,
    out_buf,
    in_buf,
    rim_send,
    rim_recv,
    *,
    halo,
):
    rows, cols = wet_ref.shape
    slots = block_ref.shape[1]
    count = rows * cols // (SUBL * LANES)
    rim = Rim(ext_ref, out_buf, in_buf, rim_send, rim_recv, rows, cols, halo)
    rim.greet()
    hit = lax.broadcasted_iota(jnp.int32, (count, slots), 0) == block_ref[...]
    hot = hit.astype(jnp.float32).astype(jnp.bfloat16)
    for i in range(SUBL):
        part = recv_ref[pl.ds(i, slots, stride=SUBL), :]
        top = part.astype(jnp.bfloat16)
        rest = (part - top.astype(jnp.float32)).astype(jnp.bfloat16)
        both = jnp.dot(
            hot, jnp.concatenate([top, rest], axis=1), preferred_element_type=jnp.float32
        )
        tile_ref[pl.ds(i, count, stride=SUBL), :] = both[:, :LANES] + both[:, LANES:]
    for c in range(cols // LANES):
        lanes = slice(c * LANES, (c + 1) * LANES)
        ext_ref[0, halo : halo + rows, lanes] = tile_ref[c * rows : (c + 1) * rows, :] * wet_ref[
            :, lanes
        ].astype(jnp.float32)
    rim.pack_columns()
    rim.start(0)
    rim.start(1)
    rim.turn()
    rim.end()


def return_kernel(told_ref, heard_ref, send_sem, recv_sem):
    width_y = lax.axis_size("gy")
    devices = lax.axis_size("gx") * width_y
    me = lax.axis_index("gx") * width_y + lax.axis_index("gy")
    greet_all(me, devices, width_y)

    def copy(p, origin):
        return pltpu.make_async_remote_copy(
            src_ref=told_ref.at[p],
            dst_ref=heard_ref.at[origin],
            send_sem=send_sem.at[p],
            recv_sem=recv_sem.at[origin],
            device_id=partner_of(p, width_y),
            device_id_type=pl.DeviceIdType.MESH,
        )

    def give(o, _):
        copy(lax.rem(me + o, devices), me).start()
        return _

    def take(o, _):
        copy(me, lax.rem(me + o, devices)).wait_recv()
        return _

    def gone(o, _):
        copy(lax.rem(me + o, devices), me).wait_send()
        return _

    lax.fori_loop(1, devices, give, 0)
    heard_ref[me] = told_ref[me]
    lax.fori_loop(1, devices, take, 0)
    lax.fori_loop(1, devices, gone, 0)


def steps_kernel(
    blocks_ref,
    grow_ref,
    gcol_ref,
    start_ref,
    static_ref,
    gauge_ref,
    recv_ref,
    final_ref,
    adjoint_ref,
    slot_ref,
    read_ref,
    face_ref,
    surf_ref,
    flux_ref,
    coef_ref,
    lam_ref,
    pick_ref,
    *,
    steps,
    halo,
    capacity,
):
    high, wide = start_ref.shape
    rows, cols = final_ref.shape
    tall = 2 * SUBL if high % (2 * SUBL) == 0 else SUBL
    strips = high // tall
    per_row = cols // LANES
    line = lax.broadcasted_iota(jnp.int32, (tall, wide), 0)

    def at(i):
        return pl.ds(pl.multiple_of(i * tall, tall), tall)

    def after(i):
        return at(jnp.minimum(i + 1, strips - 1))

    def east(x):
        return pltpu.roll(x, wide - 1, 1)

    def west(x):
        return pltpu.roll(x, 1, 1)

    def south(x, below):
        return jnp.where(line == tall - 1, pltpu.roll(below, tall - 1, 0), pltpu.roll(x, tall - 1, 0))

    def north(x, above):
        return jnp.where(line == 0, pltpu.roll(above, 1, 0), pltpu.roll(x, 1, 0))

    zero = jnp.zeros((tall, wide), jnp.float32)

    def prepare(i, _):
        here, below = at(i), after(i)
        depth, wet, fric = (static_ref[n, here, :] for n in range(3))
        depth_b, wet_b, fric_b = (static_ref[n, below, :] for n in range(3))
        face_ref[0, here, :] = 0.5 * (depth + east(depth))
        face_ref[1, here, :] = wet * east(wet)
        face_ref[2, here, :] = 0.5 * (fric + east(fric))
        face_ref[3, here, :] = 0.5 * (depth + south(depth, depth_b))
        face_ref[4, here, :] = wet * south(wet, wet_b)
        face_ref[5, here, :] = 0.5 * (fric + south(fric, fric_b))
        return _

    lax.fori_loop(0, strips, prepare, 0)

    def sweep(work, carry):
        at_once = 4

        def several(j, c):
            for n in range(at_once):
                c = work(at_once * j + n, c)
            return c

        carry = lax.fori_loop(0, strips // at_once, several, carry)
        for i in range(strips // at_once * at_once, strips):
            carry = work(i, carry)

    def face(flux, here, there, depth, wet, rough):
        raw = depth + 0.5 * (here + there)
        total = jnp.maximum(raw, min_depth)
        slope = there - here
        pushed = flux - wave_gain * total * slope
        square = pushed * pushed
        inv_speed = lax.rsqrt(square + speed_floor)
        speed = (square + speed_floor) * inv_speed
        logd = jnp.log(total)
        drag = rough * jnp.exp(logd * (-7.0 / 3.0))
        inv_depth = jnp.exp(-logd)
        ds = drag * speed
        inv = pl.reciprocal(1.0 + ds, approx=True)
        inv = inv * (2.0 - (1.0 + ds) * inv)
        wi = wet * inv
        out = wi * pushed
        d_push = wi * (1.0 - drag * square * inv_speed * inv)
        d_total = (7.0 / 3.0) * out * ds * inv * inv_depth - wave_gain * slope * d_push
        half = jnp.where(raw > min_depth, 0.5, jnp.where(raw == min_depth, 0.25, 0.0))
        both = half * d_total
        apart = wave_gain * total * d_push
        return out, d_push, apart + both, both - apart

    for k in range(steps):
        old = start_ref if k == 0 else surf_ref.at[k - 1]

        def forward(i, carry, k=k, old=old):
            cur, flux_above = carry
            here = at(i)
            nxt = old[after(i), :]
            fe = zero if k == 0 else flux_ref[0, here, :]
            fs = zero if k == 0 else flux_ref[1, here, :]
            ne, ae, xe, ye = face(
                fe, cur, east(cur), face_ref[0, here, :], face_ref[1, here, :], face_ref[2, here, :]
            )
            if k:
                coef_ref[k, 0, here, :] = ae
            coef_ref[k, 1, here, :] = xe
            coef_ref[k, 2, here, :] = ye
            ns, a_s, xs, ys = face(
                fs, cur, south(cur, nxt), face_ref[3, here, :], face_ref[4, here, :], face_ref[5, here, :]
            )
            if k:
                coef_ref[k, 3, here, :] = a_s
            coef_ref[k, 4, here, :] = xs
            coef_ref[k, 5, here, :] = ys
            if k < steps - 1:
                flux_ref[0, here, :] = ne
                flux_ref[1, here, :] = ns
            moved = ne - west(ne) + ns - north(ns, flux_above)
            surf_ref[k, here, :] = static_ref[1, here, :] * (cur - mass_gain * moved)
            return nxt, ns

        sweep(forward, (old[at(0), :], zero))

    final_ref[...] = surf_ref[steps - 1, halo : halo + rows, :cols]
    mine = grow_ref.shape[0]
    lane = lax.broadcasted_iota(jnp.int32, (mine, wide), 1)
    for k in range(steps):
        for g in range(mine):
            pick_ref[pl.ds(g, 1), :] = surf_ref[k, pl.ds(grow_ref[g], 1), :]
        hit = jnp.where(lane == gcol_ref[...], pick_ref[...], 0.0)
        read_ref[k] = jnp.broadcast_to(jnp.sum(hit, axis=1, keepdims=True), read_ref.shape[1:])

    for k in reversed(range(steps)):
        last = k == steps - 1
        src, dst = lam_ref.at[(k + 1) % 2], lam_ref.at[k % 2]

        def seeded(where, k=k, last=last, src=src):
            seed = gauge_ref[0, where, :] * surf_ref[k, where, :] - gauge_ref[1 + k, where, :]
            total = seed if last else src[where, :] + seed
            return static_ref[1, where, :] * total

        def backward(i, carry, k=k, last=last, dst=dst, seeded=seeded):
            cur, above = carry
            here = at(i)
            nxt = seeded(after(i))
            ge = -mass_gain * (cur - east(cur))
            gs = -mass_gain * (cur - south(cur, nxt))
            if not last:
                ge = ge + flux_ref[0, here, :]
                gs = gs + flux_ref[1, here, :]
            if k:
                flux_ref[0, here, :] = ge * coef_ref[k, 0, here, :]
                flux_ref[1, here, :] = gs * coef_ref[k, 3, here, :]
            ve = ge * coef_ref[k, 2, here, :]
            vs = gs * coef_ref[k, 5, here, :]
            dst[here, :] = (
                cur
                + ge * coef_ref[k, 1, here, :]
                + west(ve)
                + gs * coef_ref[k, 4, here, :]
                + north(vs, above)
            )
            return nxt, vs

        sweep(backward, (seeded(at(0)), zero))

    adjoint_ref[...] = lam_ref[0, halo : halo + rows, :cols]
    lam_ref[1, halo : halo + rows, :cols] = (
        adjoint_ref[...] * static_ref[1, halo : halo + rows, :cols]
    )

    def dots(d, _):
        for j in range(capacity):
            s = d * capacity + j
            b = blocks_ref[s]
            r = pl.multiple_of(b // per_row * SUBL + halo, SUBL)
            c = pl.multiple_of(b % per_row * LANES, LANES)
            prod = lam_ref[1, pl.ds(r, SUBL), pl.ds(c, LANES)] * recv_ref[d, j]
            slot_ref[d, pl.ds(j, 1), :] = jnp.sum(prod, axis=0, keepdims=True)
        return _

    lax.fori_loop(0, recv_ref.shape[0], dots, 0)


def body(
    ocean_depth,
    wet_mask,
    manning,
    fault_slip,
    pattern,
    foot_tile,
    foot_block,
    gauge_row,
    gauge_col,
    observed,
):
    rows, cols = ocean_depth.shape
    steps = observed.shape[0]
    halo = -(-2 * steps // SUBL) * SUBL
    wide = -(-(cols + 2 * halo) // LANES) * LANES
    high = rows + 2 * halo
    width_x = lax.axis_size("gx")
    width_y = lax.axis_size("gy")
    devices = width_x * width_y
    entries = pattern.shape[0]
    per_fault = entries // fault_slip.shape[0]
    capacity = max(2, (2 * entries + devices - 1) // devices)
    per_row = cols // LANES
    f32 = jnp.float32

    target = foot_tile[:, 0]
    order = jnp.arange(entries, dtype=jnp.int32)
    earlier = (target[:, None] == target[None, :]) & (order[:, None] > order[None, :])
    rank = jnp.sum(earlier.astype(jnp.int32), axis=1)
    place = target * capacity + rank
    weights = jnp.repeat(fault_slip, per_fault)
    slots = devices * capacity
    is_slot = place[:, None] == jnp.arange(slots, dtype=jnp.int32)[None, :]
    slot_row = jnp.sum(jnp.where(is_slot, order[:, None], 0), axis=0)
    slot_weight = jnp.sum(jnp.where(is_slot, weights[:, None], 0.0), axis=0)
    slot_block = jnp.sum(jnp.where(is_slot, foot_block[:, None], 0), axis=0).astype(f32)
    head = jnp.pad(slot_block.reshape(devices, 1, capacity), ((0, 0), (0, 0), (0, LANES - capacity)))
    here_x, here_y = lax.axis_index("gx"), lax.axis_index("gy")
    local_row = gauge_row - here_x * rows + halo
    local_col = gauge_col - here_y * cols
    local_col = jnp.where(
        (local_col < -halo) | (local_col >= cols + halo), -1, (local_col + wide) % wide
    )
    values = jnp.concatenate([jnp.ones_like(observed[:1]), observed], axis=0)
    mine = gauge_row.shape[0] // devices
    me = here_x * width_y + here_y
    my_row = lax.dynamic_slice_in_dim(local_row, me * mine, mine)
    my_col = lax.dynamic_slice_in_dim(local_col, me * mine, mine)

    vmem = pl.BlockSpec(memory_space=pltpu.VMEM)
    smem = pl.BlockSpec(memory_space=pltpu.SMEM)
    params = pltpu.CompilerParams(vmem_limit_bytes=LIMIT)

    def remote(number):
        return pltpu.CompilerParams(
            vmem_limit_bytes=LIMIT, collective_id=number, has_side_effects=True
        )

    strip = rows * halo // LANES
    four = [pltpu.SemaphoreType.DMA((4,)), pltpu.SemaphoreType.DMA((4,))]
    every = [pltpu.SemaphoreType.DMA((devices,)), pltpu.SemaphoreType.DMA((devices,))]
    recv, heads, statics, gauges = pl.pallas_call(
        partial(spread_kernel, halo=halo, capacity=capacity),
        out_shape=(
            jax.ShapeDtypeStruct((devices, capacity, SUBL, LANES), f32),
            jax.ShapeDtypeStruct((devices, 1, LANES), f32),
            jax.ShapeDtypeStruct((3, high, wide), f32),
            jax.ShapeDtypeStruct((steps + 1, high, wide), f32),
        ),
        in_specs=[smem] * 2 + [vmem] * 8,
        out_specs=(vmem,) * 4,
        scratch_shapes=[
            pltpu.VMEM((devices, capacity, SUBL, LANES), f32),
            pltpu.VMEM((2, 3, strip, LANES), f32),
            pltpu.VMEM((2, 3, strip, LANES), f32),
        ]
        + every * 2
        + four,
        compiler_params=remote(0),
    )(
        slot_row,
        slot_weight,
        pattern,
        head,
        ocean_depth,
        wet_mask,
        manning,
        local_row[None],
        local_col[None],
        values,
    )
    blocks = heads[:, 0, :capacity].astype(jnp.int32)
    number = blocks % per_row * (rows // SUBL) + blocks // per_row
    start = pl.pallas_call(
        partial(source_kernel, halo=halo),
        out_shape=jax.ShapeDtypeStruct((1, high, wide), f32),
        in_specs=[vmem] * 3,
        out_specs=vmem,
        scratch_shapes=[
            pltpu.VMEM((rows * cols // LANES, LANES), f32),
            pltpu.VMEM((2, 1, strip, LANES), f32),
            pltpu.VMEM((2, 1, strip, LANES), f32),
        ]
        + four,
        compiler_params=remote(1),
    )(number.reshape(1, slots), recv.reshape(slots * SUBL, LANES), wet_mask)[0]
    blocks = blocks.reshape(-1)
    final_eta, adjoint, per_slot, reads = pl.pallas_call(
        partial(steps_kernel, steps=steps, halo=halo, capacity=capacity),
        out_shape=(
            jax.ShapeDtypeStruct((rows, cols), f32),
            jax.ShapeDtypeStruct((rows, cols), f32),
            jax.ShapeDtypeStruct((devices, capacity, LANES), f32),
            jax.ShapeDtypeStruct((steps, mine, LANES), f32),
        ),
        in_specs=[smem, smem, vmem, vmem, vmem, vmem, vmem],
        out_specs=(vmem, vmem, vmem, vmem),
        scratch_shapes=[
            pltpu.VMEM((6, high, wide), f32),
            pltpu.VMEM((steps, high, wide), f32),
            pltpu.VMEM((2, high, wide), f32),
            pltpu.VMEM((steps, 6, high, wide), f32),
            pltpu.VMEM((2, high, wide), f32),
            pltpu.VMEM((mine, wide), f32),
        ],
        compiler_params=params,
    )(blocks, my_row, my_col[:, None], start, statics, gauges, recv)
    told = jnp.concatenate(
        [
            jnp.sum(per_slot, axis=2),
            jnp.broadcast_to(reads[:, :, 0].reshape(1, -1), (devices, steps * mine)),
        ],
        axis=1,
    )
    told = jnp.pad(told, ((0, 0), (0, -told.shape[1] % LANES)))
    heard = pl.pallas_call(
        return_kernel,
        out_shape=jax.ShapeDtypeStruct((devices, 1, told.shape[1]), f32),
        in_specs=[vmem],
        out_specs=vmem,
        scratch_shapes=every,
        compiler_params=remote(2),
    )(told[:, None, :])[:, 0]
    readings = heard[:, capacity : capacity + steps * mine].reshape(devices, steps, mine)
    readings = readings.transpose(1, 0, 2).reshape(steps, devices * mine)
    heard = heard[:, :capacity].reshape(1, -1)
    per_entry = jnp.sum(jnp.where(is_slot, heard, 0.0), axis=1)
    grad_slip = jnp.sum(per_entry.reshape(-1, per_fault), axis=1) / fault_slip
    return (final_eta, readings, adjoint, grad_slip)


def solution(mesh):
    placed = (
        P("gx", "gy"),
        P("gx", "gy"),
        P("gx", "gy"),
        P(("gx", "gy")),
        P(("gx", "gy"), None, None),
        P(("gx", "gy"), None),
        P(("gx", "gy")),
        P(),
        P(),
        P(),
    )
    return jax.shard_map(
        body,
        mesh=mesh,
        in_specs=placed,
        out_specs=(P("gx", "gy"), P(), P("gx", "gy"), P(("gx", "gy"))),
        check_vma=False,
    )
```
